32 devices in a mesh: frame: 8 (over z, y), patch: 4 (over x, core).
Axes of the slice: x: 2, y: 2, z: 4, core: 2. Of those that a mesh axis runs over, the one named last changes fastest.
Arguments:
- hidden_states: bfloat16 [8, 1024, 1152], P('frame', 'patch'), may hold values from -6 to 6
- mod_spatial: float32 [3, 1152], replicated, may hold values from -4 to 4
- w_spatial_qkv: bfloat16 [1152, 3456], P(None, 'patch'), may hold values from -2.5 to 2.5
- w_spatial_out: bfloat16 [1152, 1152], P('patch'), may hold values from -0.1875 to 0.1875
- mod_temporal: float32 [3, 1152], replicated, may hold values from -4 to 4
- w_temporal_qkv: bfloat16 [1152, 3456], P(None, 'frame'), may hold values from -2.5 to 2.5
- w_temporal_out: bfloat16 [1152, 1152], P('frame'), may hold values from -0.1875 to 0.1875
Outputs:
- block_out: bfloat16 [8, 1024, 1152], P('frame', 'patch')
The draws below stay inside these ranges and needn't reach their ends.
All inputs are finite; a program needn't handle non-finite values.
Results may differ from the reference program's by a relative error of at most 0.017.
Values may be sent and summed in bfloat16 or wider, within the bound.
No kernel may reach another device: no remote copies, remote signals or barrier semaphores. Data moves between devices by JAX's collectives and lax.ppermute only.
A program may use at most 64 MiB of HBM per device.

```python
import math
import jax
import jax.numpy as jnp
from jax import lax

D = 1152
HEADS = 16
HEAD_DIM = 72
FRAMES = 8
PATCHES = 1024


def smooth_field(key):
    keys = jax.random.split(key, 3)
    along_frames = jax.random.randint(keys[0], (D,), 1, 4).astype(jnp.float32)
    along_patches = jax.random.randint(keys[1], (D,), 1, 5).astype(jnp.float32)
    phase = jax.random.uniform(keys[2], (D,), jnp.float32, -math.pi, math.pi)
    frame_pos = jnp.arange(FRAMES, dtype=jnp.float32)[:, None, None] / FRAMES
    patch_pos = jnp.arange(PATCHES, dtype=jnp.float32)[None, :, None] / PATCHES
    return jnp.cos(2.0 * math.pi * (along_frames * frame_pos + along_patches * patch_pos) + phase)


def draw_hidden_states(key, part):
    key = jax.random.fold_in(key, 11)
    keys = jax.random.split(key, 2)
    smooth = smooth_field(keys[0])
    noise = jax.random.normal(keys[1], (FRAMES, PATCHES, D), jnp.float32)
    base = 0.85 * noise + 0.5 * smooth
    return jnp.clip(base, -6.0, 6.0).astype(jnp.bfloat16)


def projection_draw(key, spread):
    keys = jax.random.split(key, 4)
    shape = (D, HEADS, 1, HEAD_DIM)
    query = jax.random.normal(keys[0], shape, jnp.float32) / math.sqrt(D)
    other = jax.random.normal(keys[1], shape, jnp.float32) / math.sqrt(D)
    value = jax.random.normal(keys[2], shape, jnp.float32) / math.sqrt(D)
    gains = jnp.exp(jax.random.uniform(keys[3], (1, HEADS, 1, 1), jnp.float32, 0.0, spread))
    whole = jnp.concatenate([gains * query, other, value], axis=2)
    return jnp.clip(whole, -2.5, 2.5).reshape(D, 3 * D)


def draw_w_spatial_qkv(key, part):
    key = jax.random.fold_in(key, 23)
    return projection_draw(key, 0.0).astype(jnp.bfloat16)


def draw_w_temporal_qkv(key, part):
    key = jax.random.fold_in(key, 37)
    return projection_draw(key, 0.0).astype(jnp.bfloat16)


def levels(own_key, extent, cuts, low, top_value):
    gain = 1.0
    for dim, blocks in cuts:
        heights = jax.random.uniform(jax.random.fold_in(jax.random.fold_in(own_key, 6), dim), (blocks,), jnp.float32, low / len(cuts), top_value / len(cuts))
        gain = gain * jnp.repeat(jnp.exp(heights), extent[dim] // blocks).reshape((-1,) + (1,) * (len(extent) - 1 - dim))
    return gain


def normal_values(key, shape, scale, bound, cuts=(), kind=jnp.bfloat16):
    entries = scale * jax.random.normal(key, shape, jnp.float32)
    if cuts:
        entries = entries * levels(key, shape, cuts, -0.22, 0.18)
    return jnp.clip(entries, -bound, bound).astype(kind)


def setup_inputs(seed: int = 0) -> dict:
    key_list = jax.random.split(jax.random.key(seed), 8)
    return {
        "hidden_states": draw_hidden_states(jax.random.fold_in(key_list[7], 71), 0),
        "mod_spatial": normal_values(key_list[1], (3, D), 0.7, 4.0, (), jnp.float32),
        "w_spatial_qkv": draw_w_spatial_qkv(jax.random.fold_in(key_list[7], 71), 0),
        "w_spatial_out": normal_values(key_list[3], (D, D), D ** -0.5, 0.1875, ((0, 4),)),
        "mod_temporal": normal_values(key_list[4], (3, D), 0.7, 4.0, (), jnp.float32),
        "w_temporal_qkv": draw_w_temporal_qkv(jax.random.fold_in(key_list[7], 71), 0),
        "w_temporal_out": normal_values(key_list[6], (D, D), D ** -0.5, 0.1875, ((0, 8),)),
    }


EPS = 1e-06

def modulate(tokens, mod):
    values = tokens.astype(jnp.float32)
    mean = lax.optimization_barrier(jnp.mean(values, axis=-1, keepdims=True))
    centred = values - mean
    var = lax.optimization_barrier(jnp.mean(centred * centred, axis=-1, keepdims=True))
    normed = centred * lax.rsqrt(var + EPS)
    return (normed * (1.0 + mod[1]) + mod[0]).astype(jnp.bfloat16)

def project_qkv(tokens, mod, weight):
    frames, patches, width = tokens.shape
    moved = modulate(tokens, mod).reshape(frames * patches, width)
    qkv = jnp.dot(moved, weight, preferred_element_type=jnp.float32).astype(jnp.bfloat16)
    return qkv.reshape(frames, patches, HEADS, 3, HEAD_DIM)

def spatial_frame(qkv):
    query = qkv[:, :, 0].astype(jnp.float32)
    keys = qkv[:, :, 1].astype(jnp.float32)
    values = qkv[:, :, 2].astype(jnp.float32)
    scores = jnp.einsum('qhd,khd->hqk', query, keys) / math.sqrt(HEAD_DIM)
    probs = jax.nn.softmax(scores, axis=-1).astype(jnp.bfloat16)
    return jnp.einsum('hqk,khd->qhd', probs.astype(jnp.float32), values).astype(jnp.bfloat16)

def temporal_all(qkv):
    query = qkv[:, :, :, 0].astype(jnp.float32)
    keys = qkv[:, :, :, 1].astype(jnp.float32)
    values = qkv[:, :, :, 2].astype(jnp.float32)
    scores = jnp.einsum('fphd,gphd->phfg', query, keys) / math.sqrt(HEAD_DIM)
    probs = jax.nn.softmax(scores, axis=-1).astype(jnp.bfloat16)
    return jnp.einsum('phfg,gphd->fphd', probs.astype(jnp.float32), values).astype(jnp.bfloat16)

def finish(tokens, heads, mod, weight):
    frames, patches, width = tokens.shape
    flat = heads.reshape(frames * patches, width)
    update = jnp.dot(flat, weight, preferred_element_type=jnp.float32).reshape(frames, patches, width)
    return (tokens.astype(jnp.float32) + mod[2] * update).astype(jnp.bfloat16)

def reference(hidden_states, mod_spatial, w_spatial_qkv, w_spatial_out, mod_temporal, w_temporal_qkv, w_temporal_out):
    qkv = project_qkv(hidden_states, mod_spatial, w_spatial_qkv)
    heads = lax.map(spatial_frame, qkv)
    after_spatial = finish(hidden_states, heads, mod_spatial, w_spatial_out)
    qkv = project_qkv(after_spatial, mod_temporal, w_temporal_qkv)
    heads = temporal_all(qkv)
    return finish(after_spatial, heads, mod_temporal, w_temporal_out)
```

```python
import math

import jax
import jax.numpy as jnp
from jax import lax
from jax.experimental import pallas as pl
from jax.experimental.pallas import tpu as pltpu
from jax.sharding import PartitionSpec as P

HEADS = 16
HEAD_DIM = 72
PAD_DIM = 80
EPS = 1e-06
QUERY_SCALE = math.log2(math.e) / math.sqrt(HEAD_DIM)
QKV_ROWS = 224
VMEM_LIMIT = 24 * 1024 * 1024
LARGE_VMEM_LIMIT = 51 * 1024 * 1024
MEDIUM = pl.CostEstimate(flops=3 << 29, bytes_accessed=1, transcendentals=0)
SMALL = pl.CostEstimate(flops=1, bytes_accessed=1, transcendentals=0)

TRANSPOSED_RHS = (((1,), (1,)), ((), ()))
PLAIN = (((1,), (0,)), ((), ()))


def dot(lhs, rhs, dims=PLAIN):
    return lax.dot_general(lhs, rhs, dims, preferred_element_type=jnp.float32)


def normalise(tokens, mod_ref):
    values = tokens.astype(jnp.float32)
    mean = jnp.mean(values, axis=-1, keepdims=True)
    centred = values - mean
    var = jnp.mean(centred * centred, axis=-1, keepdims=True)
    normed = centred * lax.rsqrt(var + EPS)
    return (normed * (1.0 + mod_ref[1:2, :]) + mod_ref[0:1, :]).astype(jnp.bfloat16)


def split_head(columns):
    count = columns.shape[1]
    zeros = jnp.zeros((PAD_DIM - HEAD_DIM, count), jnp.float32)
    row = lax.broadcasted_iota(jnp.int32, (PAD_DIM - HEAD_DIM, count), 0)
    ones = jnp.where(row == 0, 1.0, 0.0).astype(jnp.float32)
    query = jnp.concatenate([columns[:HEAD_DIM] * QUERY_SCALE, zeros], axis=0)
    keys = jnp.concatenate([columns[HEAD_DIM : 2 * HEAD_DIM], zeros], axis=0)
    values = jnp.concatenate([columns[2 * HEAD_DIM :], ones], axis=0)
    return (
        query.astype(jnp.bfloat16),
        keys.T.astype(jnp.bfloat16),
        values.astype(jnp.bfloat16),
    )


def qkv_kernel(tokens_ref, mod_ref, weight_ref, qv_ref, keys_ref):
    moved = normalise(tokens_ref[...], mod_ref)
    columns = dot(weight_ref[...], moved, TRANSPOSED_RHS)
    for head in range(keys_ref.shape[0]):
        query, keys, values = split_head(
            columns[head * 3 * HEAD_DIM : (head + 1) * 3 * HEAD_DIM]
        )
        qv_ref[2 * head] = query
        qv_ref[2 * head + 1] = values
        keys_ref[head] = keys


def spatial_qkv(tokens, mod, weight, cost=SMALL):
    count, width = tokens.shape
    heads_here = weight.shape[0] // (3 * HEAD_DIM)
    return pl.pallas_call(
        qkv_kernel,
        out_shape=(
            jax.ShapeDtypeStruct((2 * heads_here, PAD_DIM, count), jnp.bfloat16),
            jax.ShapeDtypeStruct((heads_here, count, PAD_DIM), jnp.bfloat16),
        ),
        compiler_params=pltpu.CompilerParams(vmem_limit_bytes=VMEM_LIMIT),
        cost_estimate=cost,
        name="spatial_qkv",
    )(tokens, mod, weight)


def attention_kernel(parts, query_ref, *refs):
    qv_refs, keys_refs, out_ref, scratch = refs[:parts], refs[parts : 2 * parts], refs[-2], refs[-1]
    count = query_ref.shape[2]
    for head in range(keys_refs[0].shape[0]):
        query = query_ref[2 * head]
        scores = [dot(keys[head], query) for keys in keys_refs]
        top = jnp.max(scores[0], axis=0, keepdims=True)
        for block in scores[1:]:
            top = jnp.maximum(top, jnp.max(block, axis=0, keepdims=True))
        total = jnp.zeros((PAD_DIM, count), jnp.float32)
        for block, qv in zip(scores, qv_refs):
            probs = jnp.exp2(block - top).astype(jnp.bfloat16)
            total = total + dot(qv[2 * head + 1], probs)
        scratch[pl.ds(head * HEAD_DIM, HEAD_DIM), :] = (
            total[:HEAD_DIM] / total[HEAD_DIM : HEAD_DIM + 1]
        )
    out_ref[...] = scratch[...].T.astype(jnp.bfloat16)


def spatial_attention(query, qv_parts, keys_parts):
    heads_here, count, _ = keys_parts[0].shape
    parts = len(qv_parts)
    width = heads_here * HEAD_DIM
    return pl.pallas_call(
        lambda *refs: attention_kernel(parts, *refs),
        out_shape=jax.ShapeDtypeStruct((count, width), jnp.bfloat16),
        scratch_shapes=[pltpu.VMEM((width, count), jnp.float32)],
        compiler_params=pltpu.CompilerParams(vmem_limit_bytes=VMEM_LIMIT),
        cost_estimate=SMALL,
        name="spatial_attention",
    )(query, *qv_parts, *keys_parts)


def partial_kernel(heads_ref, other_ref, weight_ref, other_weight_ref, result_ref):
    total = dot(heads_ref[...], weight_ref[...]) + dot(other_ref[...], other_weight_ref[...])
    result_ref[...] = total.astype(jnp.bfloat16)


def chip_partial(heads, other, weight, other_weight):
    return pl.pallas_call(
        partial_kernel,
        out_shape=jax.ShapeDtypeStruct((heads.shape[0], weight.shape[1]), jnp.bfloat16),
        compiler_params=pltpu.CompilerParams(vmem_limit_bytes=VMEM_LIMIT),
        cost_estimate=SMALL,
        name="chip_partial",
    )(heads, other, weight, other_weight)


def base_kernel(tokens_ref, mod_ref, heads_ref, other_ref, weight_ref, other_weight_ref, base_ref):
    total = dot(heads_ref[...], weight_ref[...]) + dot(other_ref[...], other_weight_ref[...])
    base_ref[...] = tokens_ref[...].astype(jnp.float32) + mod_ref[2:3, :] * total


def spatial_base(tokens, mod, heads, other, weight, other_weight):
    return pl.pallas_call(
        base_kernel,
        out_shape=jax.ShapeDtypeStruct(tokens.shape, jnp.float32),
        compiler_params=pltpu.CompilerParams(vmem_limit_bytes=VMEM_LIMIT),
        cost_estimate=SMALL,
        name="spatial_base",
    )(tokens, mod, heads, other, weight, other_weight)


def add_kernel(base_ref, mod_ref, *refs):
    total = refs[0][...].astype(jnp.float32)
    for partial_ref in refs[1:-1]:
        total = total + partial_ref[...].astype(jnp.float32)
    refs[-1][...] = (base_ref[...] + mod_ref[2:3, :] * total).astype(jnp.bfloat16)


def spatial_add(base, mod, partials):
    return pl.pallas_call(
        add_kernel,
        out_shape=jax.ShapeDtypeStruct(base.shape, jnp.bfloat16),
        compiler_params=pltpu.CompilerParams(vmem_limit_bytes=VMEM_LIMIT),
        cost_estimate=MEDIUM,
        name="spatial_add",
    )(base, mod, *partials)


def pack_kernel(place_ref, qkv_ref, out_ref, *head_refs):
    count = len(head_refs)
    zeros = jnp.zeros((PAD_DIM - HEAD_DIM, qkv_ref.shape[1]), jnp.bfloat16)
    for first in range(count):

        @pl.when(place_ref[0] == first)
        def _():
            for index, head_ref in enumerate(head_refs):
                head = first ^ index
                head_ref[...] = jnp.concatenate(
                    [
                        qkv_ref[head * 3 * HEAD_DIM : (head + 1) * 3 * HEAD_DIM],
                        zeros,
                        out_ref[head * HEAD_DIM : (head + 1) * HEAD_DIM],
                        zeros,
                    ],
                    axis=0,
                )


def pack(place, qkv, out):
    count = out.shape[0] // HEAD_DIM
    if count == 1:
        place = jnp.zeros((1,), jnp.int32)
    return pl.pallas_call(
        pack_kernel,
        out_shape=(jax.ShapeDtypeStruct((QKV_ROWS + PAD_DIM, out.shape[1]), jnp.bfloat16),) * count,
        in_specs=[pl.BlockSpec(memory_space=pltpu.SMEM)]
        + [pl.BlockSpec(memory_space=pltpu.VMEM)] * 2,
        compiler_params=pltpu.CompilerParams(vmem_limit_bytes=VMEM_LIMIT),
        cost_estimate=SMALL,
        name="pack",
    )(place, qkv, out)


def temporal_kernel(positions, group, tokens_ref, moved_ref, mod_ref, *refs):
    head_refs = refs[:HEADS]
    result_ref, heads_scratch, qkv_scratch, out_scratch, sems = refs[HEADS:]
    copies = []
    for index, ref in enumerate(head_refs):
        copies.append(
            pltpu.make_async_copy(
                ref.at[pl.ds(0, QKV_ROWS)],
                qkv_scratch.at[pl.ds(index * QKV_ROWS, QKV_ROWS)],
                sems.at[index],
            )
        )
    for index, ref in enumerate(head_refs):
        copies.append(
            pltpu.make_async_copy(
                ref.at[pl.ds(QKV_ROWS, PAD_DIM)],
                out_scratch.at[pl.ds(index * PAD_DIM, PAD_DIM)],
                sems.at[HEADS + index],
            )
        )
    for copy in copies[: 2 * group]:
        copy.start()

    tokens = tokens_ref[...]
    count = tokens.shape[0]
    moved = moved_ref[...]
    key_pos = lax.broadcasted_iota(jnp.int32, (count, count), 0) % positions
    query_pos = lax.broadcasted_iota(jnp.int32, (count, count), 1) % positions
    same = key_pos == query_pos
    zeros = jnp.zeros((PAD_DIM - HEAD_DIM, count), jnp.float32)

    def project(first):
        for copy in copies[first + 2 * group : first + 3 * group]:
            copy.start()
        for index in range(first, first + group):
            copies[index].wait()
        rows = qkv_scratch[pl.ds(first * QKV_ROWS, group * QKV_ROWS), :]
        return dot(rows, moved, TRANSPOSED_RHS)

    columns = project(0)
    for first in range(0, HEADS, group):
        here = columns
        if first + group < HEADS:
            columns = project(first + group)
        split = [
            split_head(here[QKV_ROWS * k : QKV_ROWS * k + 3 * HEAD_DIM]) for k in range(group)
        ]
        scores = [jnp.where(same, dot(keys, query), -jnp.inf) for query, keys, _ in split]
        probs = [
            jnp.exp2(block - jnp.max(block, axis=0, keepdims=True)).astype(jnp.bfloat16)
            for block in scores
        ]
        mixed = [dot(values, block) for (_, _, values), block in zip(split, probs)]
        for index, block in enumerate(mixed):
            heads_scratch[pl.ds((first + index) * PAD_DIM, PAD_DIM), :] = jnp.concatenate(
                [block[:HEAD_DIM] / block[HEAD_DIM : HEAD_DIM + 1], zeros], axis=0
            )
    for copy in copies[HEADS + 2 * group :]:
        copy.start()
    for copy in copies[HEADS:]:
        copy.wait()
    total = dot(heads_scratch[...].T.astype(jnp.bfloat16), out_scratch[...])
    result_ref[...] = (tokens.astype(jnp.float32) + mod_ref[2:3, :] * total).astype(jnp.bfloat16)


def norm_kernel(tokens_ref, mod_ref, moved_ref):
    moved_ref[...] = normalise(tokens_ref[...], mod_ref)


def temporal_norm(tokens, mod):
    return pl.pallas_call(
        norm_kernel,
        out_shape=jax.ShapeDtypeStruct(tokens.shape, jnp.bfloat16),
        compiler_params=pltpu.CompilerParams(vmem_limit_bytes=VMEM_LIMIT),
        cost_estimate=SMALL,
        name="temporal_norm",
    )(tokens, mod)


def temporal_block(tokens, moved, mod, weights, positions):
    count, width = tokens.shape
    return pl.pallas_call(
        lambda *refs: temporal_kernel(positions, 2, *refs),
        out_shape=jax.ShapeDtypeStruct((count, width), jnp.bfloat16),
        in_specs=[pl.BlockSpec(memory_space=pltpu.VMEM)] * 3
        + [pl.BlockSpec(memory_space=pl.ANY)] * HEADS,
        scratch_shapes=[
            pltpu.VMEM((HEADS * PAD_DIM, count), jnp.float32),
            pltpu.VMEM((HEADS * QKV_ROWS, width), jnp.bfloat16),
            pltpu.VMEM((HEADS * PAD_DIM, width), jnp.bfloat16),
            pltpu.SemaphoreType.DMA((2 * HEADS,)),
        ],
        compiler_params=pltpu.CompilerParams(vmem_limit_bytes=LARGE_VMEM_LIMIT),
        cost_estimate=SMALL,
        name="temporal_block",
    )(tokens, moved, mod, *weights)


def swap(array, offset, count):
    return lax.ppermute(array, "patch", [(rank, rank ^ offset) for rank in range(count)])


def ring_step(array, frame_count, patch_count):
    order = list(range(0, frame_count, 2)) + list(range(1, frame_count, 2))[::-1]
    pairs = []
    for place, frame in enumerate(order):
        right, left = order[(place + 1) % frame_count], order[place - 1]
        for patch in range(patch_count):
            target = left if patch % 2 else right
            pairs.append((frame * patch_count + patch, target * patch_count + patch))
    return lax.ppermute(array, ("frame", "patch"), pairs)


def make_shards(frame_count, patch_count):
    def hop(array):
        return ring_step(array, frame_count, patch_count)

    def over_cores(array):
        return swap(array, 1, patch_count)

    def exchange(tokens):
        pieces = tokens.reshape(frame_count, -1, tokens.shape[-1])
        pieces = lax.all_to_all(pieces, "frame", 0, 0, tiled=True)
        return pieces.reshape(tokens.shape)

    def shards(
        hidden_states,
        mod_spatial,
        w_spatial_qkv,
        w_spatial_out,
        mod_temporal,
        w_temporal_qkv,
        w_temporal_out,
    ):
        _, patches, width = hidden_states.shape
        barrier = lax.optimization_barrier
        near = range(2, patch_count, 2)
        steps = frame_count // 2
        patch = lax.axis_index("patch").astype(jnp.int32)
        place = ((patch ^ (patch >> 1)) & 1).reshape(1)
        place, hidden_states = barrier((place, hidden_states))
        tokens = hidden_states.reshape(patches, width)
        w_qkv = w_spatial_qkv.T

        gathered = [tokens] * patch_count
        for offset in near:
            gathered[offset] = swap(tokens, offset, patch_count)
        gathered[1] = swap(tokens, 1, patch_count)
        weights = list(pack(place, w_temporal_qkv.T, w_temporal_out))
        first = [hop(array) for array in weights]
        other_out = over_cores(w_spatial_out)
        qkv = [None] * patch_count
        for offset in range(2):
            qkv[offset] = spatial_qkv(gathered[offset], mod_spatial, w_qkv)
        qkv[:2] = barrier(qkv[:2])
        gathered, qkv[:2] = barrier((gathered, qkv[:2]))

        for offset in near:
            gathered[offset + 1] = over_cores(gathered[offset])
        qkv[2] = spatial_qkv(gathered[2], mod_spatial, w_qkv, MEDIUM)
        qkv[2], first[0] = barrier((qkv[2], first[0]))

        second = [hop(first[0])]
        for offset in range(3, patch_count):
            qkv[offset] = spatial_qkv(gathered[offset], mod_spatial, w_qkv)
        qkv, other_out = barrier((qkv, other_out))

        qv, keys = zip(*qkv)
        heads = [None] * patch_count
        for offset in near:
            heads[offset + 1] = spatial_attention(qv[offset + 1], qv, keys)
        heads, qv, keys, first = barrier((heads, qv, keys, first))

        for offset in near:
            heads[offset + 1] = over_cores(heads[offset + 1])
            heads[offset] = spatial_attention(qv[offset], qv, keys)
        partials = [
            chip_partial(heads[offset], heads[offset + 1], w_spatial_out, other_out)
            for offset in near
        ]
        partials, qv, keys = barrier((partials, qv, keys))

        partials = [swap(partial, offset, patch_count) for partial, offset in zip(partials, near)]
        heads[1] = spatial_attention(qv[1], qv, keys)
        heads[1], qv, keys, second[0], first = barrier((heads[1], qv, keys, second[0], first))

        third = hop(second[0])
        second += [hop(array) for array in first[1:]]
        heads[0] = spatial_attention(qv[0], qv, keys)
        heads[:2] = barrier(heads[:2])

        heads[1] = over_cores(heads[1])
        base = spatial_base(tokens, mod_spatial, heads[0], heads[1], w_spatial_out, other_out)
        base, first, second[0] = barrier((base, first, second[0]))

        after_spatial = spatial_add(base, mod_spatial, partials)
        after_spatial, third = barrier((after_spatial, third))

        fourth = hop(third)
        if len(first) == 2:
            third_far = swap(third, 2, patch_count)
        arrived = exchange(after_spatial)
        moved = temporal_norm(arrived, mod_temporal)
        rest = first + second + [third]
        if len(first) == 2:
            rest += [third_far, fourth]
        else:
            for _ in range(4, steps):
                rest.append(fourth)
                fourth = hop(fourth)
            weights.append(fourth)
        for array in rest:
            weights += [array, over_cores(array)]
        result = temporal_block(arrived, moved, mod_temporal, weights, patches // frame_count)
        return exchange(result).reshape(1, patches, width)

    return shards


def solution(mesh):
    in_specs = (
        P("frame", "patch", None),
        P(),
        P(None, "patch"),
        P("patch", None),
        P(),
        P(None, "frame"),
        P("frame", None),
    )
    out_specs = P("frame", "patch", None)
    shards = make_shards(mesh.shape["frame"], mesh.shape["patch"])
    return jax.shard_map(shards, mesh=mesh, in_specs=in_specs, out_specs=out_specs, check_vma=False)
```

```python
import math

import jax
import jax.numpy as jnp
from jax import lax
from jax.experimental import pallas as pl
from jax.experimental.pallas import tpu as pltpu
from jax.sharding import PartitionSpec as P

HEADS = 16
HEAD_DIM = 72
PAD_DIM = 80
EPS = 1e-06
QUERY_SCALE = math.log2(math.e) / math.sqrt(HEAD_DIM)
HEAD_ROWS = 4 * HEAD_DIM
RESIDENT = 4
QKV_ROWS = 224
VMEM_LIMIT = 24 * 1024 * 1024
LARGE_VMEM_LIMIT = 49 * 1024 * 1024
MEDIUM = pl.CostEstimate(flops=3 << 29, bytes_accessed=1, transcendentals=0)
SMALL = pl.CostEstimate(flops=1, bytes_accessed=1, transcendentals=0)

TRANSPOSED_RHS = (((1,), (1,)), ((), ()))
PLAIN = (((1,), (0,)), ((), ()))


def dot(lhs, rhs, dims=PLAIN):
    return lax.dot_general(lhs, rhs, dims, preferred_element_type=jnp.float32)


def normalise(tokens, mod_ref):
    values = tokens.astype(jnp.float32)
    mean = jnp.mean(values, axis=-1, keepdims=True)
    centred = values - mean
    var = jnp.mean(centred * centred, axis=-1, keepdims=True)
    normed = centred * lax.rsqrt(var + EPS)
    return (normed * (1.0 + mod_ref[1:2, :]) + mod_ref[0:1, :]).astype(jnp.bfloat16)


def split_head(columns):
    count = columns.shape[1]
    zeros = jnp.zeros((PAD_DIM - HEAD_DIM, count), jnp.float32)
    row = lax.broadcasted_iota(jnp.int32, (PAD_DIM - HEAD_DIM, count), 0)
    ones = jnp.where(row == 0, 1.0, 0.0).astype(jnp.float32)
    query = jnp.concatenate([columns[:HEAD_DIM] * QUERY_SCALE, zeros], axis=0)
    keys = jnp.concatenate([columns[HEAD_DIM : 2 * HEAD_DIM], zeros], axis=0)
    values = jnp.concatenate([columns[2 * HEAD_DIM :], ones], axis=0)
    return (
        query.astype(jnp.bfloat16),
        keys.T.astype(jnp.bfloat16),
        values.astype(jnp.bfloat16),
    )


def qkv_kernel(tokens_ref, mod_ref, weight_ref, qv_ref, keys_ref):
    moved = normalise(tokens_ref[...], mod_ref)
    columns = dot(weight_ref[...], moved, TRANSPOSED_RHS)
    for head in range(keys_ref.shape[0]):
        query, keys, values = split_head(
            columns[head * 3 * HEAD_DIM : (head + 1) * 3 * HEAD_DIM]
        )
        qv_ref[2 * head] = query
        qv_ref[2 * head + 1] = values
        keys_ref[head] = keys


def spatial_qkv(tokens, mod, weight, cost=SMALL):
    count, width = tokens.shape
    heads_here = weight.shape[0] // (3 * HEAD_DIM)
    return pl.pallas_call(
        qkv_kernel,
        out_shape=(
            jax.ShapeDtypeStruct((2 * heads_here, PAD_DIM, count), jnp.bfloat16),
            jax.ShapeDtypeStruct((heads_here, count, PAD_DIM), jnp.bfloat16),
        ),
        compiler_params=pltpu.CompilerParams(vmem_limit_bytes=VMEM_LIMIT),
        cost_estimate=cost,
        name="spatial_qkv",
    )(tokens, mod, weight)


def attention_kernel(parts, query_ref, *refs):
    qv_refs, keys_refs, out_ref, scratch = refs[:parts], refs[parts : 2 * parts], refs[-2], refs[-1]
    count = query_ref.shape[2]
    for head in range(keys_refs[0].shape[0]):
        query = query_ref[2 * head]
        scores = [dot(keys[head], query) for keys in keys_refs]
        top = jnp.max(scores[0], axis=0, keepdims=True)
        for block in scores[1:]:
            top = jnp.maximum(top, jnp.max(block, axis=0, keepdims=True))
        total = jnp.zeros((PAD_DIM, count), jnp.float32)
        for block, qv in zip(scores, qv_refs):
            probs = jnp.exp2(block - top).astype(jnp.bfloat16)
            total = total + dot(qv[2 * head + 1], probs)
        scratch[pl.ds(head * HEAD_DIM, HEAD_DIM), :] = (
            total[:HEAD_DIM] / total[HEAD_DIM : HEAD_DIM + 1]
        )
    out_ref[...] = scratch[...].T.astype(jnp.bfloat16)


def spatial_attention(query, qv_parts, keys_parts):
    heads_here, count, _ = keys_parts[0].shape
    parts = len(qv_parts)
    width = heads_here * HEAD_DIM
    return pl.pallas_call(
        lambda *refs: attention_kernel(parts, *refs),
        out_shape=jax.ShapeDtypeStruct((count, width), jnp.bfloat16),
        scratch_shapes=[pltpu.VMEM((width, count), jnp.float32)],
        compiler_params=pltpu.CompilerParams(vmem_limit_bytes=VMEM_LIMIT),
        cost_estimate=SMALL,
        name="spatial_attention",
    )(query, *qv_parts, *keys_parts)


def partial_kernel(heads_ref, other_ref, weight_ref, other_weight_ref, result_ref):
    total = dot(heads_ref[...], weight_ref[...]) + dot(other_ref[...], other_weight_ref[...])
    result_ref[...] = total.astype(jnp.bfloat16)


def chip_partial(heads, other, weight, other_weight):
    return pl.pallas_call(
        partial_kernel,
        out_shape=jax.ShapeDtypeStruct((heads.shape[0], weight.shape[1]), jnp.bfloat16),
        compiler_params=pltpu.CompilerParams(vmem_limit_bytes=VMEM_LIMIT),
        cost_estimate=SMALL,
        name="chip_partial",
    )(heads, other, weight, other_weight)


def base_kernel(tokens_ref, mod_ref, heads_ref, other_ref, weight_ref, other_weight_ref, base_ref):
    total = dot(heads_ref[...], weight_ref[...]) + dot(other_ref[...], other_weight_ref[...])
    base_ref[...] = tokens_ref[...].astype(jnp.float32) + mod_ref[2:3, :] * total


def spatial_base(tokens, mod, heads, other, weight, other_weight):
    return pl.pallas_call(
        base_kernel,
        out_shape=jax.ShapeDtypeStruct(tokens.shape, jnp.float32),
        compiler_params=pltpu.CompilerParams(vmem_limit_bytes=VMEM_LIMIT),
        cost_estimate=SMALL,
        name="spatial_base",
    )(tokens, mod, heads, other, weight, other_weight)


def add_kernel(base_ref, mod_ref, *refs):
    total = refs[0][...].astype(jnp.float32)
    for partial_ref in refs[1:-1]:
        total = total + partial_ref[...].astype(jnp.float32)
    refs[-1][...] = (base_ref[...] + mod_ref[2:3, :] * total).astype(jnp.bfloat16)


def spatial_add(base, mod, partials):
    return pl.pallas_call(
        add_kernel,
        out_shape=jax.ShapeDtypeStruct(base.shape, jnp.bfloat16),
        compiler_params=pltpu.CompilerParams(vmem_limit_bytes=VMEM_LIMIT),
        cost_estimate=MEDIUM,
        name="spatial_add",
    )(base, mod, *partials)


def pack_kernel(place_ref, qkv_ref, out_ref, *head_refs):
    count = len(head_refs)
    for first in range(count):

        @pl.when(place_ref[0] == first)
        def _():
            for index, head_ref in enumerate(head_refs):
                head = first ^ index
                head_ref[...] = jnp.concatenate(
                    [
                        qkv_ref[head * 3 * HEAD_DIM : (head + 1) * 3 * HEAD_DIM],
                        out_ref[head * HEAD_DIM : (head + 1) * HEAD_DIM],
                    ],
                    axis=0,
                )


def pack(place, qkv, out):
    count = out.shape[0] // HEAD_DIM
    if count == 1:
        place = jnp.zeros((1,), jnp.int32)
    return pl.pallas_call(
        pack_kernel,
        out_shape=(jax.ShapeDtypeStruct((HEAD_ROWS, out.shape[1]), jnp.bfloat16),) * count,
        in_specs=[pl.BlockSpec(memory_space=pltpu.SMEM)]
        + [pl.BlockSpec(memory_space=pltpu.VMEM)] * 2,
        compiler_params=pltpu.CompilerParams(vmem_limit_bytes=VMEM_LIMIT),
        cost_estimate=SMALL,
        name="pack",
    )(place, qkv, out)


def temporal_kernel(positions, group, tokens_ref, moved_ref, mod_ref, *refs):
    resident_refs, streamed_refs = refs[:RESIDENT], refs[RESIDENT:HEADS]
    result_ref, heads_scratch, qkv_scratch, out_scratch, sems = refs[HEADS:]
    streamed = len(streamed_refs)
    copies = []
    for index, ref in enumerate(streamed_refs):
        copies.append(
            pltpu.make_async_copy(
                ref.at[pl.ds(0, QKV_ROWS)],
                qkv_scratch.at[pl.ds(index * QKV_ROWS, QKV_ROWS)],
                sems.at[index],
            )
        )
    for index, ref in enumerate(streamed_refs):
        copies.append(
            pltpu.make_async_copy(
                ref.at[pl.ds(HEAD_ROWS - PAD_DIM, PAD_DIM)],
                out_scratch.at[pl.ds((RESIDENT + index) * PAD_DIM, PAD_DIM)],
                sems.at[streamed + index],
            )
        )
    for copy in copies:
        copy.start()
    for index, ref in enumerate(resident_refs):
        out_scratch[pl.ds(index * PAD_DIM, PAD_DIM), :] = ref[pl.ds(HEAD_ROWS - PAD_DIM, PAD_DIM), :]

    tokens = tokens_ref[...]
    count = tokens.shape[0]
    moved = moved_ref[...]
    piece, places = by_half(count // positions, positions)
    part = count // halves_of(positions)
    key_pos = lax.broadcasted_iota(jnp.int32, (part, part), 0) % piece
    query_pos = lax.broadcasted_iota(jnp.int32, (part, part), 1) % piece
    same = key_pos == query_pos
    zeros = jnp.zeros((PAD_DIM - HEAD_DIM, count), jnp.float32)

    def project(first):
        if first < RESIDENT:
            return [
                dot(ref[pl.ds(0, QKV_ROWS), :], moved, TRANSPOSED_RHS)
                for ref in resident_refs[first : first + group]
            ]
        for copy in copies[first - RESIDENT : first - RESIDENT + group]:
            copy.wait()
        rows = qkv_scratch[pl.ds((first - RESIDENT) * QKV_ROWS, group * QKV_ROWS), :]
        columns = dot(rows, moved, TRANSPOSED_RHS)
        return [columns[QKV_ROWS * k : QKV_ROWS * (k + 1)] for k in range(group)]

    columns = project(0)
    for first in range(0, HEADS, group):
        here = columns
        if first + group < HEADS:
            columns = project(first + group)
        split = [split_head(block[: 3 * HEAD_DIM]) for block in here]
        scores = [
            jnp.where(
                same,
                dot(keys[start : start + part], query[:, start : start + part]),
                -jnp.inf,
            )
            for query, keys, _ in split
            for start in range(0, count, part)
        ]
        probs = [
            jnp.exp2(block - jnp.max(block, axis=0, keepdims=True)).astype(jnp.bfloat16)
            for block in scores
        ]
        for index, (_, _, values) in enumerate(split):
            mixed = [
                dot(values[:, start : start + part], block)
                for start, block in zip(
                    range(0, count, part), probs[index * count // part :]
                )
            ]
            block = jnp.concatenate(mixed, axis=1)
            heads_scratch[pl.ds((first + index) * PAD_DIM, PAD_DIM), :] = jnp.concatenate(
                [zeros, block[:HEAD_DIM] / block[HEAD_DIM : HEAD_DIM + 1]], axis=0
            )
    for copy in copies[streamed:]:
        copy.wait()
    total = dot(heads_scratch[...].T.astype(jnp.bfloat16), out_scratch[...])
    for start, place in places:
        result_ref[pl.ds(start, piece), :] = (
            tokens[start : start + piece].astype(jnp.float32)
            + mod_ref[2:3, :] * total[place : place + piece]
        ).astype(jnp.bfloat16)


def halves_of(positions):
    return 1 if positions % 32 else 2


def by_half(frames, positions):
    halves = halves_of(positions)
    rows = positions // halves
    return rows, [
        (frame * positions + half * rows, (half * frames + frame) * rows)
        for half in range(halves)
        for frame in range(frames)
    ]


def norm_kernel(positions, tokens_ref, mod_ref, moved_ref):
    moved = normalise(tokens_ref[...], mod_ref)
    rows, places = by_half(moved.shape[0] // positions, positions)
    for start, place in places:
        moved_ref[pl.ds(place, rows), :] = moved[start : start + rows]


def temporal_norm(tokens, mod, positions):
    return pl.pallas_call(
        lambda *refs: norm_kernel(positions, *refs),
        out_shape=jax.ShapeDtypeStruct(tokens.shape, jnp.bfloat16),
        compiler_params=pltpu.CompilerParams(vmem_limit_bytes=VMEM_LIMIT),
        cost_estimate=SMALL,
        name="temporal_norm",
    )(tokens, mod)


def temporal_block(tokens, moved, mod, weights, positions):
    count, width = tokens.shape
    return pl.pallas_call(
        lambda *refs: temporal_kernel(positions, 4, *refs),
        out_shape=jax.ShapeDtypeStruct((count, width), jnp.bfloat16),
        in_specs=[pl.BlockSpec(memory_space=pltpu.VMEM)] * (3 + RESIDENT)
        + [pl.BlockSpec(memory_space=pl.ANY)] * (HEADS - RESIDENT),
        scratch_shapes=[
            pltpu.VMEM((HEADS * PAD_DIM, count), jnp.float32),
            pltpu.VMEM(((HEADS - RESIDENT) * QKV_ROWS, width), jnp.bfloat16),
            pltpu.VMEM((HEADS * PAD_DIM, width), jnp.bfloat16),
            pltpu.SemaphoreType.DMA((2 * (HEADS - RESIDENT),)),
        ],
        compiler_params=pltpu.CompilerParams(vmem_limit_bytes=LARGE_VMEM_LIMIT),
        cost_estimate=SMALL,
        name="temporal_block",
    )(tokens, moved, mod, *weights)


def swap(array, offset, count):
    return lax.ppermute(array, "patch", [(rank, rank ^ offset) for rank in range(count)])


def ring_step(array, frame_count, patch_count):
    order = list(range(0, frame_count, 2)) + list(range(1, frame_count, 2))[::-1]
    pairs = []
    for place, frame in enumerate(order):
        right, left = order[(place + 1) % frame_count], order[place - 1]
        for patch in range(patch_count):
            target = left if patch % 2 else right
            pairs.append((frame * patch_count + patch, target * patch_count + patch))
    return lax.ppermute(array, ("frame", "patch"), pairs)


def make_shards(frame_count, patch_count):
    def hop(array):
        return ring_step(array, frame_count, patch_count)

    def over_cores(array):
        return swap(array, 1, patch_count)

    def exchange(tokens):
        pieces = tokens.reshape(frame_count, -1, tokens.shape[-1])
        pieces = lax.all_to_all(pieces, "frame", 0, 0, tiled=True)
        return pieces.reshape(tokens.shape)

    def shards(
        hidden_states,
        mod_spatial,
        w_spatial_qkv,
        w_spatial_out,
        mod_temporal,
        w_temporal_qkv,
        w_temporal_out,
    ):
        _, patches, width = hidden_states.shape
        barrier = lax.optimization_barrier
        near = range(2, patch_count, 2)
        steps = frame_count // 2
        patch = lax.axis_index("patch").astype(jnp.int32)
        place = ((patch ^ (patch >> 1)) & 1).reshape(1)
        place, hidden_states = barrier((place, hidden_states))
        tokens = hidden_states.reshape(patches, width)
        w_qkv = w_spatial_qkv.T

        gathered = [tokens] * patch_count
        for offset in near:
            gathered[offset] = swap(tokens, offset, patch_count)
        gathered[1] = swap(tokens, 1, patch_count)
        weights = list(pack(place, w_temporal_qkv.T, w_temporal_out))
        first = [hop(array) for array in weights]
        other_out = over_cores(w_spatial_out)
        qkv = [None] * patch_count
        for offset in range(2):
            qkv[offset] = spatial_qkv(gathered[offset], mod_spatial, w_qkv)
        qkv[:2] = barrier(qkv[:2])
        gathered, qkv[:2] = barrier((gathered, qkv[:2]))

        for offset in near:
            gathered[offset + 1] = over_cores(gathered[offset])
        qkv[2] = spatial_qkv(gathered[2], mod_spatial, w_qkv, MEDIUM)
        qkv[2], first[0] = barrier((qkv[2], first[0]))

        second = [hop(first[0])]
        for offset in range(3, patch_count):
            qkv[offset] = spatial_qkv(gathered[offset], mod_spatial, w_qkv)
        qkv, other_out = barrier((qkv, other_out))

        qv, keys = zip(*qkv)
        heads = [None] * patch_count
        for offset in near:
            heads[offset + 1] = spatial_attention(qv[offset + 1], qv, keys)
        heads, qv, keys, first = barrier((heads, qv, keys, first))

        for offset in near:
            heads[offset + 1] = over_cores(heads[offset + 1])
            heads[offset] = spatial_attention(qv[offset], qv, keys)
        partials = [
            chip_partial(heads[offset], heads[offset + 1], w_spatial_out, other_out)
            for offset in near
        ]
        partials, qv, keys = barrier((partials, qv, keys))

        partials = [swap(partial, offset, patch_count) for partial, offset in zip(partials, near)]
        heads[1] = spatial_attention(qv[1], qv, keys)
        heads[1], qv, keys, second[0], first = barrier((heads[1], qv, keys, second[0], first))

        third = hop(second[0])
        second += [hop(array) for array in first[1:]]
        heads[0] = spatial_attention(qv[0], qv, keys)
        heads[:2] = barrier(heads[:2])

        heads[1] = over_cores(heads[1])
        base = spatial_base(tokens, mod_spatial, heads[0], heads[1], w_spatial_out, other_out)
        base, first, second[0] = barrier((base, first, second[0]))

        after_spatial = spatial_add(base, mod_spatial, partials)
        after_spatial, third = barrier((after_spatial, third))

        fourth = hop(third)
        if len(first) == 2:
            third_far = swap(third, 2, patch_count)
        arrived = exchange(after_spatial)
        moved = temporal_norm(arrived, mod_temporal, patches // frame_count)
        weights += first
        others = [over_cores(array) for array in first]
        rest = second + [third]
        if len(first) == 2:
            rest += [third_far, fourth]
        else:
            for _ in range(4, steps):
                rest.append(fourth)
                fourth = hop(fourth)
            weights.append(fourth)
        for array in rest:
            others += [array, over_cores(array)]
        weights += others
        result = temporal_block(arrived, moved, mod_temporal, weights, patches // frame_count)
        return exchange(result).reshape(1, patches, width)

    return shards


def solution(mesh):
    in_specs = (
        P("frame", "patch", None),
        P(),
        P(None, "patch"),
        P("patch", None),
        P(),
        P(None, "frame"),
        P("frame", None),
    )
    out_specs = P("frame", "patch", None)
    shards = make_shards(mesh.shape["frame"], mesh.shape["patch"])
    return jax.shard_map(shards, mesh=mesh, in_specs=in_specs, out_specs=out_specs, check_vma=False)
```

```python
import math

import jax
import jax.numpy as jnp
from jax import lax
from jax.experimental import pallas as pl
from jax.experimental.pallas import tpu as pltpu
from jax.sharding import PartitionSpec as P

HEADS = 16
HEAD_DIM = 72
PAD_DIM = 80
EPS = 1e-06
QUERY_SCALE = math.log2(math.e) / math.sqrt(HEAD_DIM)
HEAD_ROWS = 4 * HEAD_DIM
RESIDENT = 4
QKV_ROWS = 224
VMEM_LIMIT = 24 * 1024 * 1024
LARGE_VMEM_LIMIT = 49 * 1024 * 1024
MEDIUM = pl.CostEstimate(flops=3 << 29, bytes_accessed=1, transcendentals=0)
SMALL = pl.CostEstimate(flops=1, bytes_accessed=1, transcendentals=0)

TRANSPOSED_RHS = (((1,), (1,)), ((), ()))
PLAIN = (((1,), (0,)), ((), ()))


def dot(lhs, rhs, dims=PLAIN):
    return lax.dot_general(lhs, rhs, dims, preferred_element_type=jnp.float32)


def normalise(tokens, mod_ref):
    values = tokens.astype(jnp.float32)
    mean = jnp.mean(values, axis=-1, keepdims=True)
    centred = values - mean
    var = jnp.mean(centred * centred, axis=-1, keepdims=True)
    normed = centred * lax.rsqrt(var + EPS)
    return (normed * (1.0 + mod_ref[1:2, :]) + mod_ref[0:1, :]).astype(jnp.bfloat16)


def split_head(columns):
    count = columns.shape[1]
    zeros = jnp.zeros((PAD_DIM - HEAD_DIM, count), jnp.float32)
    row = lax.broadcasted_iota(jnp.int32, (PAD_DIM - HEAD_DIM, count), 0)
    ones = jnp.where(row == 0, 1.0, 0.0).astype(jnp.float32)
    query = jnp.concatenate([columns[:HEAD_DIM] * QUERY_SCALE, zeros], axis=0)
    keys = jnp.concatenate([columns[HEAD_DIM : 2 * HEAD_DIM], zeros], axis=0)
    values = jnp.concatenate([columns[2 * HEAD_DIM :], ones], axis=0)
    return (
        query.astype(jnp.bfloat16),
        keys.T.astype(jnp.bfloat16),
        values.astype(jnp.bfloat16),
    )


def qkv_kernel(tokens_ref, mod_ref, weight_ref, qv_ref, keys_ref):
    moved = normalise(tokens_ref[...], mod_ref)
    columns = dot(weight_ref[...], moved, TRANSPOSED_RHS)
    for head in range(keys_ref.shape[0]):
        query, keys, values = split_head(
            columns[head * 3 * HEAD_DIM : (head + 1) * 3 * HEAD_DIM]
        )
        qv_ref[2 * head] = query
        qv_ref[2 * head + 1] = values
        keys_ref[head] = keys


def spatial_qkv(tokens, mod, weight, cost=SMALL):
    count, width = tokens.shape
    heads_here = weight.shape[0] // (3 * HEAD_DIM)
    return pl.pallas_call(
        qkv_kernel,
        out_shape=(
            jax.ShapeDtypeStruct((2 * heads_here, PAD_DIM, count), jnp.bfloat16),
            jax.ShapeDtypeStruct((heads_here, count, PAD_DIM), jnp.bfloat16),
        ),
        compiler_params=pltpu.CompilerParams(vmem_limit_bytes=VMEM_LIMIT),
        cost_estimate=cost,
        name="spatial_qkv",
    )(tokens, mod, weight)


def attention_kernel(parts, query_ref, *refs):
    qv_refs, keys_refs, out_ref, scratch = refs[:parts], refs[parts : 2 * parts], refs[-2], refs[-1]
    count = query_ref.shape[2]
    for head in range(keys_refs[0].shape[0]):
        query = query_ref[2 * head]
        scores = [dot(keys[head], query) for keys in keys_refs]
        top = jnp.max(scores[0], axis=0, keepdims=True)
        for block in scores[1:]:
            top = jnp.maximum(top, jnp.max(block, axis=0, keepdims=True))
        total = jnp.zeros((PAD_DIM, count), jnp.float32)
        for block, qv in zip(scores, qv_refs):
            probs = jnp.exp2(block - top).astype(jnp.bfloat16)
            total = total + dot(qv[2 * head + 1], probs)
        scratch[pl.ds(head * HEAD_DIM, HEAD_DIM), :] = (
            total[:HEAD_DIM] / total[HEAD_DIM : HEAD_DIM + 1]
        )
    out_ref[...] = scratch[...].T.astype(jnp.bfloat16)


def spatial_attention(query, qv_parts, keys_parts):
    heads_here, count, _ = keys_parts[0].shape
    parts = len(qv_parts)
    width = heads_here * HEAD_DIM
    return pl.pallas_call(
        lambda *refs: attention_kernel(parts, *refs),
        out_shape=jax.ShapeDtypeStruct((count, width), jnp.bfloat16),
        scratch_shapes=[pltpu.VMEM((width, count), jnp.float32)],
        compiler_params=pltpu.CompilerParams(vmem_limit_bytes=VMEM_LIMIT),
        cost_estimate=SMALL,
        name="spatial_attention",
    )(query, *qv_parts, *keys_parts)


def partial_kernel(heads_ref, other_ref, weight_ref, other_weight_ref, result_ref):
    total = dot(heads_ref[...], weight_ref[...]) + dot(other_ref[...], other_weight_ref[...])
    result_ref[...] = total.astype(jnp.bfloat16)


def chip_partial(heads, other, weight, other_weight):
    return pl.pallas_call(
        partial_kernel,
        out_shape=jax.ShapeDtypeStruct((heads.shape[0], weight.shape[1]), jnp.bfloat16),
        compiler_params=pltpu.CompilerParams(vmem_limit_bytes=VMEM_LIMIT),
        cost_estimate=SMALL,
        name="chip_partial",
    )(heads, other, weight, other_weight)


def base_kernel(tokens_ref, mod_ref, heads_ref, other_ref, weight_ref, other_weight_ref, base_ref):
    total = dot(heads_ref[...], weight_ref[...]) + dot(other_ref[...], other_weight_ref[...])
    base_ref[...] = tokens_ref[...].astype(jnp.float32) + mod_ref[2:3, :] * total


def spatial_base(tokens, mod, heads, other, weight, other_weight):
    return pl.pallas_call(
        base_kernel,
        out_shape=jax.ShapeDtypeStruct(tokens.shape, jnp.float32),
        compiler_params=pltpu.CompilerParams(vmem_limit_bytes=VMEM_LIMIT),
        cost_estimate=SMALL,
        name="spatial_base",
    )(tokens, mod, heads, other, weight, other_weight)


def add_kernel(base_ref, mod_ref, *refs):
    total = refs[0][...].astype(jnp.float32)
    for partial_ref in refs[1:-1]:
        total = total + partial_ref[...].astype(jnp.float32)
    refs[-1][...] = (base_ref[...] + mod_ref[2:3, :] * total).astype(jnp.bfloat16)


def spatial_add(base, mod, partials):
    return pl.pallas_call(
        add_kernel,
        out_shape=jax.ShapeDtypeStruct(base.shape, jnp.bfloat16),
        compiler_params=pltpu.CompilerParams(vmem_limit_bytes=VMEM_LIMIT),
        cost_estimate=MEDIUM,
        name="spatial_add",
    )(base, mod, *partials)


def pack_kernel(place_ref, qkv_ref, out_ref, *head_refs):
    count = len(head_refs)
    for first in range(count):

        @pl.when(place_ref[0] == first)
        def _():
            for index, head_ref in enumerate(head_refs):
                head = first ^ index
                head_ref[...] = jnp.concatenate(
                    [
                        qkv_ref[head * 3 * HEAD_DIM : (head + 1) * 3 * HEAD_DIM],
                        out_ref[head * HEAD_DIM : (head + 1) * HEAD_DIM],
                    ],
                    axis=0,
                )


def pack(place, qkv, out):
    count = out.shape[0] // HEAD_DIM
    if count == 1:
        place = jnp.zeros((1,), jnp.int32)
    return pl.pallas_call(
        pack_kernel,
        out_shape=(jax.ShapeDtypeStruct((HEAD_ROWS, out.shape[1]), jnp.bfloat16),) * count,
        in_specs=[pl.BlockSpec(memory_space=pltpu.SMEM)]
        + [pl.BlockSpec(memory_space=pltpu.VMEM)] * 2,
        compiler_params=pltpu.CompilerParams(vmem_limit_bytes=VMEM_LIMIT),
        cost_estimate=SMALL,
        name="pack",
    )(place, qkv, out)


def frame_start(frame_ref, offset, positions):
    return pl.multiple_of((frame_ref[0] ^ offset) * positions, positions)


def temporal_kernel(positions, group, frame_ref, tokens_ref, moved_ref, mod_ref, *refs):
    resident_refs, streamed_refs = refs[:RESIDENT], refs[RESIDENT:HEADS]
    *piece_refs, result_ref, heads_scratch, qkv_scratch, out_scratch, sems = refs[HEADS:]
    streamed = len(streamed_refs)
    copies = []
    for index, ref in enumerate(streamed_refs):
        copies.append(
            pltpu.make_async_copy(
                ref.at[pl.ds(0, QKV_ROWS)],
                qkv_scratch.at[pl.ds(index * QKV_ROWS, QKV_ROWS)],
                sems.at[index],
            )
        )
    for index, ref in enumerate(streamed_refs):
        copies.append(
            pltpu.make_async_copy(
                ref.at[pl.ds(HEAD_ROWS - PAD_DIM, PAD_DIM)],
                out_scratch.at[pl.ds((RESIDENT + index) * PAD_DIM, PAD_DIM)],
                sems.at[streamed + index],
            )
        )
    for copy in copies:
        copy.start()
    for index, ref in enumerate(resident_refs):
        out_scratch[pl.ds(index * PAD_DIM, PAD_DIM), :] = ref[pl.ds(HEAD_ROWS - PAD_DIM, PAD_DIM), :]

    tokens = tokens_ref[...]
    count = tokens.shape[0]
    moved = moved_ref[...]
    piece, places = by_half(count // positions, positions)
    part = count // halves_of(positions)
    key_pos = lax.broadcasted_iota(jnp.int32, (part, part), 0) % piece
    query_pos = lax.broadcasted_iota(jnp.int32, (part, part), 1) % piece
    same = key_pos == query_pos
    zeros = jnp.zeros((PAD_DIM - HEAD_DIM, count), jnp.float32)

    def project(first):
        if first < RESIDENT:
            return [
                dot(ref[pl.ds(0, QKV_ROWS), :], moved, TRANSPOSED_RHS)
                for ref in resident_refs[first : first + group]
            ]
        for copy in copies[first - RESIDENT : first - RESIDENT + group]:
            copy.wait()
        rows = qkv_scratch[pl.ds((first - RESIDENT) * QKV_ROWS, group * QKV_ROWS), :]
        columns = dot(rows, moved, TRANSPOSED_RHS)
        return [columns[QKV_ROWS * k : QKV_ROWS * (k + 1)] for k in range(group)]

    columns = project(0)
    for first in range(0, HEADS, group):
        here = columns
        if first + group < HEADS:
            columns = project(first + group)
        split = [split_head(block[: 3 * HEAD_DIM]) for block in here]
        scores = [
            jnp.where(
                same,
                dot(keys[start : start + part], query[:, start : start + part]),
                -jnp.inf,
            )
            for query, keys, _ in split
            for start in range(0, count, part)
        ]
        probs = [
            jnp.exp2(block - jnp.max(block, axis=0, keepdims=True)).astype(jnp.bfloat16)
            for block in scores
        ]
        for index, (_, _, values) in enumerate(split):
            mixed = [
                dot(values[:, start : start + part], block)
                for start, block in zip(
                    range(0, count, part), probs[index * count // part :]
                )
            ]
            block = jnp.concatenate(mixed, axis=1)
            heads_scratch[pl.ds((first + index) * PAD_DIM, PAD_DIM), :] = jnp.concatenate(
                [zeros, block[:HEAD_DIM] / block[HEAD_DIM : HEAD_DIM + 1]], axis=0
            )
    for copy in copies[streamed:]:
        copy.wait()
    total = dot(heads_scratch[...].T.astype(jnp.bfloat16), out_scratch[...])
    for start, place in places:
        result_ref[pl.ds(start, piece), :] = (
            tokens[start : start + piece].astype(jnp.float32)
            + mod_ref[2:3, :] * total[place : place + piece]
        )
    for offset, piece_ref in enumerate(piece_refs):
        start = frame_start(frame_ref, offset, positions)
        piece_ref[...] = result_ref[pl.ds(start, positions), :].astype(jnp.bfloat16)


def halves_of(positions):
    return 1 if positions % 32 else 2


def by_half(frames, positions):
    halves = halves_of(positions)
    rows = positions // halves
    return rows, [
        (frame * positions + half * rows, (half * frames + frame) * rows)
        for half in range(halves)
        for frame in range(frames)
    ]


def norm_kernel(positions, tokens_ref, mod_ref, moved_ref):
    moved = normalise(tokens_ref[...], mod_ref)
    rows, places = by_half(moved.shape[0] // positions, positions)
    for start, place in places:
        moved_ref[pl.ds(place, rows), :] = moved[start : start + rows]


def temporal_norm(tokens, mod, positions):
    return pl.pallas_call(
        lambda *refs: norm_kernel(positions, *refs),
        out_shape=jax.ShapeDtypeStruct(tokens.shape, jnp.bfloat16),
        compiler_params=pltpu.CompilerParams(vmem_limit_bytes=VMEM_LIMIT),
        cost_estimate=SMALL,
        name="temporal_norm",
    )(tokens, mod)


def temporal_block(frame, tokens, moved, mod, weights, positions):
    count, width = tokens.shape
    return pl.pallas_call(
        lambda *refs: temporal_kernel(positions, 4, *refs),
        out_shape=(jax.ShapeDtypeStruct((positions, width), jnp.bfloat16),) * (count // positions),
        in_specs=[pl.BlockSpec(memory_space=pltpu.SMEM)]
        + [pl.BlockSpec(memory_space=pltpu.VMEM)] * (3 + RESIDENT)
        + [pl.BlockSpec(memory_space=pl.ANY)] * (HEADS - RESIDENT),
        scratch_shapes=[
            pltpu.VMEM((count, width), jnp.float32),
            pltpu.VMEM((HEADS * PAD_DIM, count), jnp.float32),
            pltpu.VMEM(((HEADS - RESIDENT) * QKV_ROWS, width), jnp.bfloat16),
            pltpu.VMEM((HEADS * PAD_DIM, width), jnp.bfloat16),
            pltpu.SemaphoreType.DMA((2 * (HEADS - RESIDENT),)),
        ],
        compiler_params=pltpu.CompilerParams(vmem_limit_bytes=LARGE_VMEM_LIMIT),
        cost_estimate=SMALL,
        name="temporal_block",
    )(frame, tokens, moved, mod, *weights)


def join_kernel(offsets, frame_ref, *refs):
    positions = refs[0].shape[0]
    for offset, ref in zip(offsets, refs[:-1]):
        refs[-1][pl.ds(frame_start(frame_ref, offset, positions), positions), :] = ref[...]


def join_frames(frame, pieces, offsets):
    positions, width = pieces[0].shape
    return pl.pallas_call(
        lambda *refs: join_kernel(offsets, *refs),
        out_shape=jax.ShapeDtypeStruct((positions * len(pieces), width), jnp.bfloat16),
        in_specs=[pl.BlockSpec(memory_space=pltpu.SMEM)]
        + [pl.BlockSpec(memory_space=pltpu.VMEM)] * len(pieces),
        compiler_params=pltpu.CompilerParams(vmem_limit_bytes=VMEM_LIMIT),
        cost_estimate=SMALL,
        name="join_frames",
    )(frame, *pieces)


def swap(array, offset, count):
    return lax.ppermute(array, "patch", [(rank, rank ^ offset) for rank in range(count)])


def frame_swap(array, offset, count):
    return lax.ppermute(array, "frame", [(rank, rank ^ offset) for rank in range(count)])


def ring_step(array, frame_count, patch_count):
    order = list(range(0, frame_count, 2)) + list(range(1, frame_count, 2))[::-1]
    pairs = []
    for place, frame in enumerate(order):
        right, left = order[(place + 1) % frame_count], order[place - 1]
        for patch in range(patch_count):
            target = left if patch % 2 else right
            pairs.append((frame * patch_count + patch, target * patch_count + patch))
    return lax.ppermute(array, ("frame", "patch"), pairs)


def make_shards(frame_count, patch_count):
    def hop(array):
        return ring_step(array, frame_count, patch_count)

    def over_cores(array):
        return swap(array, 1, patch_count)

    def exchange(tokens):
        pieces = tokens.reshape(frame_count, -1, tokens.shape[-1])
        pieces = lax.all_to_all(pieces, "frame", 0, 0, tiled=True)
        return pieces.reshape(tokens.shape)

    def shards(
        hidden_states,
        mod_spatial,
        w_spatial_qkv,
        w_spatial_out,
        mod_temporal,
        w_temporal_qkv,
        w_temporal_out,
    ):
        _, patches, width = hidden_states.shape
        barrier = lax.optimization_barrier
        near = range(2, patch_count, 2)
        steps = frame_count // 2
        patch = lax.axis_index("patch").astype(jnp.int32)
        place = ((patch ^ (patch >> 1)) & 1).reshape(1)
        frame = lax.axis_index("frame").astype(jnp.int32).reshape(1)
        place, frame, hidden_states = barrier((place, frame, hidden_states))
        tokens = hidden_states.reshape(patches, width)
        w_qkv = w_spatial_qkv.T

        gathered = [tokens] * patch_count
        for offset in near:
            gathered[offset] = swap(tokens, offset, patch_count)
        gathered[1] = swap(tokens, 1, patch_count)
        weights = list(pack(place, w_temporal_qkv.T, w_temporal_out))
        first = [hop(array) for array in weights]
        other_out = over_cores(w_spatial_out)
        qkv = [None] * patch_count
        for offset in range(2):
            qkv[offset] = spatial_qkv(gathered[offset], mod_spatial, w_qkv)
        qkv[:2] = barrier(qkv[:2])
        gathered, qkv[:2] = barrier((gathered, qkv[:2]))

        for offset in near:
            gathered[offset + 1] = over_cores(gathered[offset])
        qkv[2] = spatial_qkv(gathered[2], mod_spatial, w_qkv, MEDIUM)
        qkv[2], first[0] = barrier((qkv[2], first[0]))

        second = [hop(first[0])]
        for offset in range(3, patch_count):
            qkv[offset] = spatial_qkv(gathered[offset], mod_spatial, w_qkv)
        qkv, other_out = barrier((qkv, other_out))

        qv, keys = zip(*qkv)
        heads = [None] * patch_count
        for offset in near:
            heads[offset + 1] = spatial_attention(qv[offset + 1], qv, keys)
        heads, qv, keys, first = barrier((heads, qv, keys, first))

        for offset in near:
            heads[offset + 1] = over_cores(heads[offset + 1])
            heads[offset] = spatial_attention(qv[offset], qv, keys)
        partials = [
            chip_partial(heads[offset], heads[offset + 1], w_spatial_out, other_out)
            for offset in near
        ]
        partials, qv, keys = barrier((partials, qv, keys))

        partials = [swap(partial, offset, patch_count) for partial, offset in zip(partials, near)]
        heads[1] = spatial_attention(qv[1], qv, keys)
        heads[1], qv, keys, second[0], first = barrier((heads[1], qv, keys, second[0], first))

        third = hop(second[0])
        second += [hop(array) for array in first[1:]]
        heads[0] = spatial_attention(qv[0], qv, keys)
        heads[:2] = barrier(heads[:2])

        heads[1] = over_cores(heads[1])
        base = spatial_base(tokens, mod_spatial, heads[0], heads[1], w_spatial_out, other_out)
        base, first, second[0] = barrier((base, first, second[0]))

        after_spatial = spatial_add(base, mod_spatial, partials)
        after_spatial, third = barrier((after_spatial, third))

        fourth = hop(third)
        if len(first) == 2:
            third_far = swap(third, 2, patch_count)
        arrived = exchange(after_spatial)
        moved = temporal_norm(arrived, mod_temporal, patches // frame_count)
        weights += first
        others = [over_cores(array) for array in first]
        rest = second + [third]
        if len(first) == 2:
            rest += [third_far, fourth]
        else:
            for _ in range(4, steps):
                rest.append(fourth)
                fourth = hop(fourth)
            weights.append(fourth)
        for array in rest:
            others += [array, over_cores(array)]
        weights += others
        positions = patches // frame_count
        pieces = list(temporal_block(frame, arrived, moved, mod_temporal, weights, positions))
        middle = frame_count // 2
        far = list(range(middle, frame_count))
        order = [0, *far[:2], 1, *far[2:], *range(2, middle)]
        for offset in order[1:]:
            pieces[offset] = frame_swap(pieces[offset], offset, frame_count)
        result = join_frames(frame, [pieces[offset] for offset in order], order)
        return result.reshape(1, patches, width)

    return shards


def solution(mesh):
    in_specs = (
        P("frame", "patch", None),
        P(),
        P(None, "patch"),
        P("patch", None),
        P(),
        P(None, "frame"),
        P("frame", None),
    )
    out_specs = P("frame", "patch", None)
    shards = make_shards(mesh.shape["frame"], mesh.shape["patch"])
    return jax.shard_map(shards, mesh=mesh, in_specs=in_specs, out_specs=out_specs, check_vma=False)
```

```python
import math

import jax
import jax.numpy as jnp
from jax import lax
from jax.experimental import pallas as pl
from jax.experimental.pallas import tpu as pltpu
from jax.sharding import PartitionSpec as P

HEADS = 16
HEAD_DIM = 72
PAD_DIM = 80
EPS = 1e-06
QUERY_SCALE = math.log2(math.e) / math.sqrt(HEAD_DIM)
HEAD_ROWS = 4 * HEAD_DIM
RESIDENT = 4
QKV_ROWS = 224
VMEM_LIMIT = 24 * 1024 * 1024
LARGE_VMEM_LIMIT = 49 * 1024 * 1024
MEDIUM = pl.CostEstimate(flops=3 << 29, bytes_accessed=1, transcendentals=0)
SMALL = pl.CostEstimate(flops=1, bytes_accessed=1, transcendentals=0)

TRANSPOSED_RHS = (((1,), (1,)), ((), ()))
PLAIN = (((1,), (0,)), ((), ()))


def dot(lhs, rhs, dims=PLAIN):
    return lax.dot_general(lhs, rhs, dims, preferred_element_type=jnp.float32)


def normalise(tokens, mod_ref):
    values = tokens.astype(jnp.float32)
    mean = jnp.mean(values, axis=-1, keepdims=True)
    centred = values - mean
    var = jnp.mean(centred * centred, axis=-1, keepdims=True)
    normed = centred * lax.rsqrt(var + EPS)
    return (normed * (1.0 + mod_ref[1:2, :]) + mod_ref[0:1, :]).astype(jnp.bfloat16)


def split_head(columns):
    count = columns.shape[1]
    zeros = jnp.zeros((PAD_DIM - HEAD_DIM, count), jnp.float32)
    row = lax.broadcasted_iota(jnp.int32, (PAD_DIM - HEAD_DIM, count), 0)
    ones = jnp.where(row == 0, 1.0, 0.0).astype(jnp.float32)
    query = jnp.concatenate([columns[:HEAD_DIM] * QUERY_SCALE, zeros], axis=0)
    keys = jnp.concatenate([columns[HEAD_DIM : 2 * HEAD_DIM], zeros], axis=0)
    values = jnp.concatenate([columns[2 * HEAD_DIM :], ones], axis=0)
    return (
        query.astype(jnp.bfloat16),
        keys.T.astype(jnp.bfloat16),
        values.astype(jnp.bfloat16),
    )


def qkv_kernel(tokens_ref, mod_ref, weight_ref, qv_ref, keys_ref):
    moved = normalise(tokens_ref[...], mod_ref)
    columns = dot(weight_ref[...], moved, TRANSPOSED_RHS)
    for head in range(keys_ref.shape[0]):
        query, keys, values = split_head(
            columns[head * 3 * HEAD_DIM : (head + 1) * 3 * HEAD_DIM]
        )
        qv_ref[2 * head] = query
        qv_ref[2 * head + 1] = values
        keys_ref[head] = keys


def spatial_qkv(tokens, mod, weight, cost=SMALL):
    count, width = tokens.shape
    heads_here = weight.shape[0] // (3 * HEAD_DIM)
    return pl.pallas_call(
        qkv_kernel,
        out_shape=(
            jax.ShapeDtypeStruct((2 * heads_here, PAD_DIM, count), jnp.bfloat16),
            jax.ShapeDtypeStruct((heads_here, count, PAD_DIM), jnp.bfloat16),
        ),
        compiler_params=pltpu.CompilerParams(vmem_limit_bytes=VMEM_LIMIT),
        cost_estimate=cost,
        name="spatial_qkv",
    )(tokens, mod, weight)


def attention_kernel(parts, query_ref, *refs):
    qv_refs, keys_refs, out_ref, scratch = refs[:parts], refs[parts : 2 * parts], refs[-2], refs[-1]
    count = query_ref.shape[2]
    for head in range(keys_refs[0].shape[0]):
        query = query_ref[2 * head]
        scores = [dot(keys[head], query) for keys in keys_refs]
        top = jnp.max(scores[0], axis=0, keepdims=True)
        for block in scores[1:]:
            top = jnp.maximum(top, jnp.max(block, axis=0, keepdims=True))
        total = jnp.zeros((PAD_DIM, count), jnp.float32)
        for block, qv in zip(scores, qv_refs):
            probs = jnp.exp2(block - top).astype(jnp.bfloat16)
            total = total + dot(qv[2 * head + 1], probs)
        scratch[pl.ds(head * HEAD_DIM, HEAD_DIM), :] = (
            total[:HEAD_DIM] / total[HEAD_DIM : HEAD_DIM + 1]
        )
    out_ref[...] = scratch[...].T.astype(jnp.bfloat16)


def spatial_attention(query, qv_parts, keys_parts):
    heads_here, count, _ = keys_parts[0].shape
    parts = len(qv_parts)
    width = heads_here * HEAD_DIM
    return pl.pallas_call(
        lambda *refs: attention_kernel(parts, *refs),
        out_shape=jax.ShapeDtypeStruct((count, width), jnp.bfloat16),
        scratch_shapes=[pltpu.VMEM((width, count), jnp.float32)],
        compiler_params=pltpu.CompilerParams(vmem_limit_bytes=VMEM_LIMIT),
        cost_estimate=SMALL,
        name="spatial_attention",
    )(query, *qv_parts, *keys_parts)


def partial_kernel(heads_ref, other_ref, weight_ref, other_weight_ref, result_ref):
    total = dot(heads_ref[...], weight_ref[...]) + dot(other_ref[...], other_weight_ref[...])
    result_ref[...] = total.astype(jnp.bfloat16)


def chip_partial(heads, other, weight, other_weight):
    return pl.pallas_call(
        partial_kernel,
        out_shape=jax.ShapeDtypeStruct((heads.shape[0], weight.shape[1]), jnp.bfloat16),
        compiler_params=pltpu.CompilerParams(vmem_limit_bytes=VMEM_LIMIT),
        cost_estimate=SMALL,
        name="chip_partial",
    )(heads, other, weight, other_weight)


def base_kernel(tokens_ref, mod_ref, heads_ref, other_ref, weight_ref, other_weight_ref, base_ref):
    total = dot(heads_ref[...], weight_ref[...]) + dot(other_ref[...], other_weight_ref[...])
    base_ref[...] = tokens_ref[...].astype(jnp.float32) + mod_ref[2:3, :] * total


def spatial_base(tokens, mod, heads, other, weight, other_weight):
    return pl.pallas_call(
        base_kernel,
        out_shape=jax.ShapeDtypeStruct(tokens.shape, jnp.float32),
        compiler_params=pltpu.CompilerParams(vmem_limit_bytes=VMEM_LIMIT),
        cost_estimate=SMALL,
        name="spatial_base",
    )(tokens, mod, heads, other, weight, other_weight)


def add_kernel(base_ref, mod_ref, *refs):
    total = refs[0][...].astype(jnp.float32)
    for partial_ref in refs[1:-1]:
        total = total + partial_ref[...].astype(jnp.float32)
    refs[-1][...] = (base_ref[...] + mod_ref[2:3, :] * total).astype(jnp.bfloat16)


def spatial_add(base, mod, partials):
    return pl.pallas_call(
        add_kernel,
        out_shape=jax.ShapeDtypeStruct(base.shape, jnp.bfloat16),
        compiler_params=pltpu.CompilerParams(vmem_limit_bytes=VMEM_LIMIT),
        cost_estimate=MEDIUM,
        name="spatial_add",
    )(base, mod, *partials)


def pack_kernel(place_ref, qkv_ref, out_ref, *head_refs):
    count = len(head_refs)
    for first in range(count):

        @pl.when(place_ref[0] == first)
        def _():
            for index, head_ref in enumerate(head_refs):
                head = first ^ index
                head_ref[...] = jnp.concatenate(
                    [
                        qkv_ref[head * 3 * HEAD_DIM : (head + 1) * 3 * HEAD_DIM],
                        out_ref[head * HEAD_DIM : (head + 1) * HEAD_DIM],
                    ],
                    axis=0,
                )


def pack(place, qkv, out):
    count = out.shape[0] // HEAD_DIM
    if count == 1:
        place = jnp.zeros((1,), jnp.int32)
    return pl.pallas_call(
        pack_kernel,
        out_shape=(jax.ShapeDtypeStruct((HEAD_ROWS, out.shape[1]), jnp.bfloat16),) * count,
        in_specs=[pl.BlockSpec(memory_space=pltpu.SMEM)]
        + [pl.BlockSpec(memory_space=pltpu.VMEM)] * 2,
        compiler_params=pltpu.CompilerParams(vmem_limit_bytes=VMEM_LIMIT),
        cost_estimate=SMALL,
        name="pack",
    )(place, qkv, out)


def frame_start(frame_ref, offset, positions):
    return pl.multiple_of((frame_ref[0] ^ offset) * positions, positions)


def temporal_kernel(positions, group, frame_ref, tokens_ref, moved_ref, mod_ref, *refs):
    resident_refs, streamed_refs = refs[:RESIDENT], refs[RESIDENT:HEADS]
    *piece_refs, result_ref, heads_scratch, qkv_scratch, out_scratch, sems = refs[HEADS:]
    streamed = len(streamed_refs)
    copies = []
    for index, ref in enumerate(streamed_refs):
        copies.append(
            pltpu.make_async_copy(
                ref.at[pl.ds(0, QKV_ROWS)],
                qkv_scratch.at[pl.ds(index * QKV_ROWS, QKV_ROWS)],
                sems.at[index],
            )
        )
    for index, ref in enumerate(streamed_refs):
        copies.append(
            pltpu.make_async_copy(
                ref.at[pl.ds(HEAD_ROWS - PAD_DIM, PAD_DIM)],
                out_scratch.at[pl.ds((RESIDENT + index) * PAD_DIM, PAD_DIM)],
                sems.at[streamed + index],
            )
        )
    for copy in copies:
        copy.start()
    for index, ref in enumerate(resident_refs):
        out_scratch[pl.ds(index * PAD_DIM, PAD_DIM), :] = ref[pl.ds(HEAD_ROWS - PAD_DIM, PAD_DIM), :]

    tokens = tokens_ref[...]
    count = tokens.shape[0]
    moved = moved_ref[...]
    piece, places = by_half(count // positions, positions)
    part = count // halves_of(positions)
    key_pos = lax.broadcasted_iota(jnp.int32, (part, part), 0) % piece
    query_pos = lax.broadcasted_iota(jnp.int32, (part, part), 1) % piece
    same = key_pos == query_pos
    zeros = jnp.zeros((PAD_DIM - HEAD_DIM, count), jnp.float32)

    def project(first):
        if first < RESIDENT:
            return [
                dot(ref[pl.ds(0, QKV_ROWS), :], moved, TRANSPOSED_RHS)
                for ref in resident_refs[first : first + group]
            ]
        for copy in copies[first - RESIDENT : first - RESIDENT + group]:
            copy.wait()
        rows = qkv_scratch[pl.ds((first - RESIDENT) * QKV_ROWS, group * QKV_ROWS), :]
        columns = dot(rows, moved, TRANSPOSED_RHS)
        return [columns[QKV_ROWS * k : QKV_ROWS * (k + 1)] for k in range(group)]

    columns = project(0)
    for first in range(0, HEADS, group):
        here = columns
        if first + group < HEADS:
            columns = project(first + group)
        split = [split_head(block[: 3 * HEAD_DIM]) for block in here]
        scores = [
            jnp.where(
                same,
                dot(keys[start : start + part], query[:, start : start + part]),
                -jnp.inf,
            )
            for query, keys, _ in split
            for start in range(0, count, part)
        ]
        probs = [
            jnp.exp2(block - jnp.max(block, axis=0, keepdims=True)).astype(jnp.bfloat16)
            for block in scores
        ]
        for index, (_, _, values) in enumerate(split):
            mixed = [
                dot(values[:, start : start + part], block)
                for start, block in zip(
                    range(0, count, part), probs[index * count // part :]
                )
            ]
            block = jnp.concatenate(mixed, axis=1)
            heads_scratch[pl.ds((first + index) * PAD_DIM, PAD_DIM), :] = jnp.concatenate(
                [zeros, block[:HEAD_DIM] / block[HEAD_DIM : HEAD_DIM + 1]], axis=0
            )
    for copy in copies[streamed:]:
        copy.wait()
    total = dot(heads_scratch[...].T.astype(jnp.bfloat16), out_scratch[...])
    for start, place in places:
        result_ref[pl.ds(start, piece), :] = (
            tokens[start : start + piece].astype(jnp.float32)
            + mod_ref[2:3, :] * total[place : place + piece]
        )
    for offset, piece_ref in enumerate(piece_refs):
        start = frame_start(frame_ref, offset, positions)
        piece_ref[...] = result_ref[pl.ds(start, positions), :].astype(jnp.bfloat16)


def halves_of(positions):
    return 1 if positions % 32 else 2


def by_half(frames, positions):
    halves = halves_of(positions)
    rows = positions // halves
    return rows, [
        (frame * positions + half * rows, (half * frames + frame) * rows)
        for half in range(halves)
        for frame in range(frames)
    ]


def norm_kernel(positions, tokens_ref, mod_ref, moved_ref):
    moved = normalise(tokens_ref[...], mod_ref)
    rows, places = by_half(moved.shape[0] // positions, positions)
    for start, place in places:
        moved_ref[pl.ds(place, rows), :] = moved[start : start + rows]


def temporal_norm(tokens, mod, positions):
    return pl.pallas_call(
        lambda *refs: norm_kernel(positions, *refs),
        out_shape=jax.ShapeDtypeStruct(tokens.shape, jnp.bfloat16),
        compiler_params=pltpu.CompilerParams(vmem_limit_bytes=VMEM_LIMIT),
        cost_estimate=SMALL,
        name="temporal_norm",
    )(tokens, mod)


def temporal_block(frame, tokens, moved, mod, weights, positions):
    count, width = tokens.shape
    return pl.pallas_call(
        lambda *refs: temporal_kernel(positions, 4, *refs),
        out_shape=(jax.ShapeDtypeStruct((positions, width), jnp.bfloat16),) * (count // positions),
        in_specs=[pl.BlockSpec(memory_space=pltpu.SMEM)]
        + [pl.BlockSpec(memory_space=pltpu.VMEM)] * (3 + RESIDENT)
        + [pl.BlockSpec(memory_space=pl.ANY)] * (HEADS - RESIDENT),
        scratch_shapes=[
            pltpu.VMEM((count, width), jnp.float32),
            pltpu.VMEM((HEADS * PAD_DIM, count), jnp.float32),
            pltpu.VMEM(((HEADS - RESIDENT) * QKV_ROWS, width), jnp.bfloat16),
            pltpu.VMEM((HEADS * PAD_DIM, width), jnp.bfloat16),
            pltpu.SemaphoreType.DMA((2 * (HEADS - RESIDENT),)),
        ],
        compiler_params=pltpu.CompilerParams(vmem_limit_bytes=LARGE_VMEM_LIMIT),
        cost_estimate=SMALL,
        name="temporal_block",
    )(frame, tokens, moved, mod, *weights)


def join_kernel(offsets, frame_ref, *refs):
    positions = refs[0].shape[0]
    for offset, ref in zip(offsets, refs[:-1]):
        refs[-1][pl.ds(frame_start(frame_ref, offset, positions), positions), :] = ref[...]


def join_frames(frame, pieces, offsets):
    positions, width = pieces[0].shape
    return pl.pallas_call(
        lambda *refs: join_kernel(offsets, *refs),
        out_shape=jax.ShapeDtypeStruct((positions * len(pieces), width), jnp.bfloat16),
        in_specs=[pl.BlockSpec(memory_space=pltpu.SMEM)]
        + [pl.BlockSpec(memory_space=pltpu.VMEM)] * len(pieces),
        compiler_params=pltpu.CompilerParams(vmem_limit_bytes=VMEM_LIMIT),
        cost_estimate=SMALL,
        name="join_frames",
    )(frame, *pieces)


def swap(array, offset, count):
    return lax.ppermute(array, "patch", [(rank, rank ^ offset) for rank in range(count)])


def frame_swap(array, offset, count):
    return lax.ppermute(array, "frame", [(rank, rank ^ offset) for rank in range(count)])


def ring_step(array, frame_count, patch_count):
    order = list(range(0, frame_count, 2)) + list(range(1, frame_count, 2))[::-1]
    pairs = []
    for place, frame in enumerate(order):
        right, left = order[(place + 1) % frame_count], order[place - 1]
        for patch in range(patch_count):
            target = left if patch % 2 else right
            pairs.append((frame * patch_count + patch, target * patch_count + patch))
    return lax.ppermute(array, ("frame", "patch"), pairs)


def make_shards(frame_count, patch_count):
    def hop(array):
        return ring_step(array, frame_count, patch_count)

    def over_cores(array):
        return swap(array, 1, patch_count)

    def exchange(tokens):
        pieces = tokens.reshape(frame_count, -1, tokens.shape[-1])
        pieces = lax.all_to_all(pieces, "frame", 0, 0, tiled=True)
        return pieces.reshape(tokens.shape)

    def shards(
        hidden_states,
        mod_spatial,
        w_spatial_qkv,
        w_spatial_out,
        mod_temporal,
        w_temporal_qkv,
        w_temporal_out,
    ):
        _, patches, width = hidden_states.shape
        barrier = lax.optimization_barrier
        near = range(2, patch_count, 2)
        steps = frame_count // 2
        patch = lax.axis_index("patch").astype(jnp.int32)
        place = ((patch ^ (patch >> 1)) & 1).reshape(1)
        frame = lax.axis_index("frame").astype(jnp.int32).reshape(1)
        place, frame, hidden_states = barrier((place, frame, hidden_states))
        tokens = hidden_states.reshape(patches, width)
        w_qkv = w_spatial_qkv.T

        gathered = [tokens] * patch_count
        for offset in near:
            gathered[offset] = swap(tokens, offset, patch_count)
        gathered[1] = swap(tokens, 1, patch_count)
        weights = list(pack(place, w_temporal_qkv.T, w_temporal_out))
        first = [hop(array) for array in weights]
        other_out = over_cores(w_spatial_out)
        qkv = [None] * patch_count
        for offset in range(2):
            qkv[offset] = spatial_qkv(gathered[offset], mod_spatial, w_qkv)
        qkv[:2] = barrier(qkv[:2])
        gathered, qkv[:2] = barrier((gathered, qkv[:2]))

        for offset in near:
            gathered[offset + 1] = over_cores(gathered[offset])
        qkv[2] = spatial_qkv(gathered[2], mod_spatial, w_qkv, MEDIUM)
        qkv[2], first[0] = barrier((qkv[2], first[0]))

        second = [hop(first[0])]
        for offset in range(3, patch_count):
            qkv[offset] = spatial_qkv(gathered[offset], mod_spatial, w_qkv)
        qkv, other_out = barrier((qkv, other_out))

        qv, keys = zip(*qkv)
        heads = [None] * patch_count
        for offset in near:
            heads[offset + 1] = spatial_attention(qv[offset + 1], qv, keys)
        heads, qv, keys, first = barrier((heads, qv, keys, first))

        for offset in near:
            heads[offset + 1] = over_cores(heads[offset + 1])
            heads[offset] = spatial_attention(qv[offset], qv, keys)
        partials = [
            chip_partial(heads[offset], heads[offset + 1], w_spatial_out, other_out)
            for offset in near
        ]
        partials, qv, keys = barrier((partials, qv, keys))

        partials = [swap(partial, offset, patch_count) for partial, offset in zip(partials, near)]
        heads[1] = spatial_attention(qv[1], qv, keys)
        heads[1], qv, keys, second[0], first = barrier((heads[1], qv, keys, second[0], first))

        third = hop(second[0])
        second += [hop(array) for array in first[1:]]
        heads[0] = spatial_attention(qv[0], qv, keys)
        heads[:2] = barrier(heads[:2])

        heads[1] = over_cores(heads[1])
        base = spatial_base(tokens, mod_spatial, heads[0], heads[1], w_spatial_out, other_out)
        base, first, second[0] = barrier((base, first, second[0]))

        after_spatial = spatial_add(base, mod_spatial, partials)
        after_spatial, third = barrier((after_spatial, third))

        fourth = hop(third)
        if len(first) == 2:
            third_far = swap(third, 2, patch_count)
        arrived = exchange(after_spatial)
        moved = temporal_norm(arrived, mod_temporal, patches // frame_count)
        weights += first
        others = [over_cores(array) for array in first]
        rest = second + [third]
        if len(first) == 2:
            rest += [third_far, fourth]
        else:
            for _ in range(4, steps):
                rest.append(fourth)
                fourth = hop(fourth)
            weights.append(fourth)
        for array in rest:
            others += [array, over_cores(array)]
        weights += others
        positions = patches // frame_count
        pieces = list(temporal_block(frame, arrived, moved, mod_temporal, weights, positions))
        middle = frame_count // 2
        far = [*range(middle * 3 // 2, frame_count), *range(middle, middle * 3 // 2)]
        order = [0, 1, far[0], 2, *far[1:], *range(3, middle)]
        for offset in order[1:]:
            pieces[offset] = frame_swap(pieces[offset], offset, frame_count)
        result = join_frames(frame, [pieces[offset] for offset in order], order)
        return result.reshape(1, patches, width)

    return shards


def solution(mesh):
    in_specs = (
        P("frame", "patch", None),
        P(),
        P(None, "patch"),
        P("patch", None),
        P(),
        P(None, "frame"),
        P("frame", None),
    )
    out_specs = P("frame", "patch", None)
    shards = make_shards(mesh.shape["frame"], mesh.shape["patch"])
    return jax.shard_map(shards, mesh=mesh, in_specs=in_specs, out_specs=out_specs, check_vma=False)
```

```python
import math

import jax
import jax.numpy as jnp
from jax import lax
from jax.experimental import pallas as pl
from jax.experimental.pallas import tpu as pltpu
from jax.sharding import PartitionSpec as P

HEADS = 16
HEAD_DIM = 72
PAD_DIM = 80
EPS = 1e-06
QUERY_SCALE = math.log2(math.e) / math.sqrt(HEAD_DIM)
HEAD_ROWS = 4 * HEAD_DIM
RESIDENT = 4
QKV_ROWS = 224
VMEM_LIMIT = 24 * 1024 * 1024
LARGE_VMEM_LIMIT = 49 * 1024 * 1024
MEDIUM = pl.CostEstimate(flops=3 << 29, bytes_accessed=1, transcendentals=0)
SMALL = pl.CostEstimate(flops=1, bytes_accessed=1, transcendentals=0)

TRANSPOSED_RHS = (((1,), (1,)), ((), ()))
PLAIN = (((1,), (0,)), ((), ()))


def dot(lhs, rhs, dims=PLAIN):
    return lax.dot_general(lhs, rhs, dims, preferred_element_type=jnp.float32)


def normalise(tokens, mod_ref):
    values = tokens.astype(jnp.float32)
    mean = jnp.mean(values, axis=-1, keepdims=True)
    centred = values - mean
    var = jnp.mean(centred * centred, axis=-1, keepdims=True)
    normed = centred * lax.rsqrt(var + EPS)
    return (normed * (1.0 + mod_ref[1:2, :]) + mod_ref[0:1, :]).astype(jnp.bfloat16)


def split_head(columns):
    count = columns.shape[1]
    zeros = jnp.zeros((PAD_DIM - HEAD_DIM, count), jnp.float32)
    row = lax.broadcasted_iota(jnp.int32, (PAD_DIM - HEAD_DIM, count), 0)
    ones = jnp.where(row == 0, 1.0, 0.0).astype(jnp.float32)
    query = jnp.concatenate([columns[:HEAD_DIM] * QUERY_SCALE, zeros], axis=0)
    keys = jnp.concatenate([columns[HEAD_DIM : 2 * HEAD_DIM], zeros], axis=0)
    values = jnp.concatenate([columns[2 * HEAD_DIM :], ones], axis=0)
    return (
        query.astype(jnp.bfloat16),
        keys.T.astype(jnp.bfloat16),
        values.astype(jnp.bfloat16),
    )


def qkv_kernel(tokens_ref, mod_ref, weight_ref, qv_ref, keys_ref):
    moved = normalise(tokens_ref[...], mod_ref)
    columns = dot(weight_ref[...], moved, TRANSPOSED_RHS)
    for head in range(keys_ref.shape[0]):
        query, keys, values = split_head(
            columns[head * 3 * HEAD_DIM : (head + 1) * 3 * HEAD_DIM]
        )
        qv_ref[2 * head] = query
        qv_ref[2 * head + 1] = values
        keys_ref[head] = keys


def spatial_qkv(tokens, mod, weight, cost=SMALL):
    count, width = tokens.shape
    heads_here = weight.shape[0] // (3 * HEAD_DIM)
    return pl.pallas_call(
        qkv_kernel,
        out_shape=(
            jax.ShapeDtypeStruct((2 * heads_here, PAD_DIM, count), jnp.bfloat16),
            jax.ShapeDtypeStruct((heads_here, count, PAD_DIM), jnp.bfloat16),
        ),
        compiler_params=pltpu.CompilerParams(vmem_limit_bytes=VMEM_LIMIT),
        cost_estimate=cost,
        name="spatial_qkv",
    )(tokens, mod, weight)


def attention_kernel(parts, query_ref, *refs):
    qv_refs, keys_refs, out_ref, scratch = refs[:parts], refs[parts : 2 * parts], refs[-2], refs[-1]
    count = query_ref.shape[2]
    for head in range(keys_refs[0].shape[0]):
        query = query_ref[2 * head]
        scores = [dot(keys[head], query) for keys in keys_refs]
        top = jnp.max(scores[0], axis=0, keepdims=True)
        for block in scores[1:]:
            top = jnp.maximum(top, jnp.max(block, axis=0, keepdims=True))
        total = jnp.zeros((PAD_DIM, count), jnp.float32)
        for block, qv in zip(scores, qv_refs):
            probs = jnp.exp2(block - top).astype(jnp.bfloat16)
            total = total + dot(qv[2 * head + 1], probs)
        scratch[pl.ds(head * HEAD_DIM, HEAD_DIM), :] = (
            total[:HEAD_DIM] / total[HEAD_DIM : HEAD_DIM + 1]
        )
    out_ref[...] = scratch[...].T.astype(jnp.bfloat16)


def spatial_attention(query, qv_parts, keys_parts):
    heads_here, count, _ = keys_parts[0].shape
    parts = len(qv_parts)
    width = heads_here * HEAD_DIM
    return pl.pallas_call(
        lambda *refs: attention_kernel(parts, *refs),
        out_shape=jax.ShapeDtypeStruct((count, width), jnp.bfloat16),
        scratch_shapes=[pltpu.VMEM((width, count), jnp.float32)],
        compiler_params=pltpu.CompilerParams(vmem_limit_bytes=VMEM_LIMIT),
        cost_estimate=SMALL,
        name="spatial_attention",
    )(query, *qv_parts, *keys_parts)


def partial_kernel(heads_ref, other_ref, weight_ref, other_weight_ref, result_ref):
    total = dot(heads_ref[...], weight_ref[...]) + dot(other_ref[...], other_weight_ref[...])
    result_ref[...] = total.astype(jnp.bfloat16)


def chip_partial(heads, other, weight, other_weight):
    return pl.pallas_call(
        partial_kernel,
        out_shape=jax.ShapeDtypeStruct((heads.shape[0], weight.shape[1]), jnp.bfloat16),
        compiler_params=pltpu.CompilerParams(vmem_limit_bytes=VMEM_LIMIT),
        cost_estimate=SMALL,
        name="chip_partial",
    )(heads, other, weight, other_weight)


def base_kernel(tokens_ref, mod_ref, heads_ref, other_ref, weight_ref, other_weight_ref, base_ref):
    total = dot(heads_ref[...], weight_ref[...]) + dot(other_ref[...], other_weight_ref[...])
    base_ref[...] = tokens_ref[...].astype(jnp.float32) + mod_ref[2:3, :] * total


def spatial_base(tokens, mod, heads, other, weight, other_weight):
    return pl.pallas_call(
        base_kernel,
        out_shape=jax.ShapeDtypeStruct(tokens.shape, jnp.float32),
        compiler_params=pltpu.CompilerParams(vmem_limit_bytes=VMEM_LIMIT),
        cost_estimate=SMALL,
        name="spatial_base",
    )(tokens, mod, heads, other, weight, other_weight)


def add_kernel(base_ref, mod_ref, *refs):
    total = refs[0][...].astype(jnp.float32)
    for partial_ref in refs[1:-1]:
        total = total + partial_ref[...].astype(jnp.float32)
    refs[-1][...] = (base_ref[...] + mod_ref[2:3, :] * total).astype(jnp.bfloat16)


def spatial_add(base, mod, partials):
    return pl.pallas_call(
        add_kernel,
        out_shape=jax.ShapeDtypeStruct(base.shape, jnp.bfloat16),
        compiler_params=pltpu.CompilerParams(vmem_limit_bytes=VMEM_LIMIT),
        cost_estimate=MEDIUM,
        name="spatial_add",
    )(base, mod, *partials)


def pack_kernel(place_ref, qkv_ref, out_ref, *head_refs):
    count = len(head_refs)
    for first in range(count):

        @pl.when(place_ref[0] == first)
        def _():
            for index, head_ref in enumerate(head_refs):
                head = first ^ index
                head_ref[...] = jnp.concatenate(
                    [
                        qkv_ref[head * 3 * HEAD_DIM : (head + 1) * 3 * HEAD_DIM],
                        out_ref[head * HEAD_DIM : (head + 1) * HEAD_DIM],
                    ],
                    axis=0,
                )


def pack(place, qkv, out):
    count = out.shape[0] // HEAD_DIM
    if count == 1:
        place = jnp.zeros((1,), jnp.int32)
    return pl.pallas_call(
        pack_kernel,
        out_shape=(jax.ShapeDtypeStruct((HEAD_ROWS, out.shape[1]), jnp.bfloat16),) * count,
        in_specs=[pl.BlockSpec(memory_space=pltpu.SMEM)]
        + [pl.BlockSpec(memory_space=pltpu.VMEM)] * 2,
        compiler_params=pltpu.CompilerParams(vmem_limit_bytes=VMEM_LIMIT),
        cost_estimate=SMALL,
        name="pack",
    )(place, qkv, out)


def frame_start(frame_ref, offset, positions):
    return pl.multiple_of((frame_ref[0] ^ offset) * positions, positions)


def temporal_kernel(positions, group, frame_ref, tokens_ref, moved_ref, mod_ref, *refs):
    resident_refs, streamed_refs = refs[:RESIDENT], refs[RESIDENT:HEADS]
    *piece_refs, result_ref, heads_scratch, qkv_scratch, out_scratch, sems = refs[HEADS:]
    streamed = len(streamed_refs)
    copies = []
    for index, ref in enumerate(streamed_refs):
        copies.append(
            pltpu.make_async_copy(
                ref.at[pl.ds(0, QKV_ROWS)],
                qkv_scratch.at[pl.ds(index * QKV_ROWS, QKV_ROWS)],
                sems.at[index],
            )
        )
    for index, ref in enumerate(streamed_refs):
        copies.append(
            pltpu.make_async_copy(
                ref.at[pl.ds(HEAD_ROWS - PAD_DIM, PAD_DIM)],
                out_scratch.at[pl.ds((RESIDENT + index) * PAD_DIM, PAD_DIM)],
                sems.at[streamed + index],
            )
        )
    for copy in copies:
        copy.start()
    for index, ref in enumerate(resident_refs):
        out_scratch[pl.ds(index * PAD_DIM, PAD_DIM), :] = ref[pl.ds(HEAD_ROWS - PAD_DIM, PAD_DIM), :]

    tokens = tokens_ref[...]
    count = tokens.shape[0]
    moved = moved_ref[...]
    piece, places = by_half(count // positions, positions)
    part = count // halves_of(positions)
    key_pos = lax.broadcasted_iota(jnp.int32, (part, part), 0) % piece
    query_pos = lax.broadcasted_iota(jnp.int32, (part, part), 1) % piece
    same = key_pos == query_pos
    zeros = jnp.zeros((PAD_DIM - HEAD_DIM, count), jnp.float32)

    def project(first):
        if first < RESIDENT:
            return [
                dot(ref[pl.ds(0, QKV_ROWS), :], moved, TRANSPOSED_RHS)
                for ref in resident_refs[first : first + group]
            ]
        for copy in copies[first - RESIDENT : first - RESIDENT + group]:
            copy.wait()
        rows = qkv_scratch[pl.ds((first - RESIDENT) * QKV_ROWS, group * QKV_ROWS), :]
        columns = dot(rows, moved, TRANSPOSED_RHS)
        return [columns[QKV_ROWS * k : QKV_ROWS * (k + 1)] for k in range(group)]

    columns = project(0)
    for first in range(0, HEADS, group):
        here = columns
        if first + group < HEADS:
            columns = project(first + group)
        split = [split_head(block[: 3 * HEAD_DIM]) for block in here]
        scores = [
            jnp.where(
                same,
                dot(keys[start : start + part], query[:, start : start + part]),
                -jnp.inf,
            )
            for query, keys, _ in split
            for start in range(0, count, part)
        ]
        probs = [
            jnp.exp2(block - jnp.max(block, axis=0, keepdims=True)).astype(jnp.bfloat16)
            for block in scores
        ]
        for index, (_, _, values) in enumerate(split):
            mixed = [
                dot(values[:, start : start + part], block)
                for start, block in zip(
                    range(0, count, part), probs[index * count // part :]
                )
            ]
            block = jnp.concatenate(mixed, axis=1)
            heads_scratch[pl.ds((first + index) * PAD_DIM, PAD_DIM), :] = jnp.concatenate(
                [zeros, block[:HEAD_DIM] / block[HEAD_DIM : HEAD_DIM + 1]], axis=0
            )
    for copy in copies[streamed:]:
        copy.wait()
    total = dot(heads_scratch[...].T.astype(jnp.bfloat16), out_scratch[...])
    for start, place in places:
        result_ref[pl.ds(start, piece), :] = (
            tokens[start : start + piece].astype(jnp.float32)
            + mod_ref[2:3, :] * total[place : place + piece]
        )
    for offset, piece_ref in enumerate(piece_refs):
        start = frame_start(frame_ref, offset, positions)
        piece_ref[...] = result_ref[pl.ds(start, positions), :].astype(jnp.bfloat16)


def halves_of(positions):
    return 1 if positions % 32 else 2


def by_half(frames, positions):
    halves = halves_of(positions)
    rows = positions // halves
    return rows, [
        (frame * positions + half * rows, (half * frames + frame) * rows)
        for half in range(halves)
        for frame in range(frames)
    ]


def norm_kernel(positions, tokens_ref, mod_ref, moved_ref):
    moved = normalise(tokens_ref[...], mod_ref)
    rows, places = by_half(moved.shape[0] // positions, positions)
    for start, place in places:
        moved_ref[pl.ds(place, rows), :] = moved[start : start + rows]


def temporal_norm(tokens, mod, positions):
    return pl.pallas_call(
        lambda *refs: norm_kernel(positions, *refs),
        out_shape=jax.ShapeDtypeStruct(tokens.shape, jnp.bfloat16),
        compiler_params=pltpu.CompilerParams(vmem_limit_bytes=VMEM_LIMIT),
        cost_estimate=SMALL,
        name="temporal_norm",
    )(tokens, mod)


def temporal_block(frame, tokens, moved, mod, weights, positions):
    count, width = tokens.shape
    return pl.pallas_call(
        lambda *refs: temporal_kernel(positions, 4, *refs),
        out_shape=(jax.ShapeDtypeStruct((positions, width), jnp.bfloat16),) * (count // positions),
        in_specs=[pl.BlockSpec(memory_space=pltpu.SMEM)]
        + [pl.BlockSpec(memory_space=pltpu.VMEM)] * (3 + RESIDENT)
        + [pl.BlockSpec(memory_space=pl.ANY)] * (HEADS - RESIDENT),
        scratch_shapes=[
            pltpu.VMEM((count, width), jnp.float32),
            pltpu.VMEM((HEADS * PAD_DIM, count), jnp.float32),
            pltpu.VMEM(((HEADS - RESIDENT) * QKV_ROWS, width), jnp.bfloat16),
            pltpu.VMEM((HEADS * PAD_DIM, width), jnp.bfloat16),
            pltpu.SemaphoreType.DMA((2 * (HEADS - RESIDENT),)),
        ],
        compiler_params=pltpu.CompilerParams(vmem_limit_bytes=LARGE_VMEM_LIMIT),
        cost_estimate=SMALL,
        name="temporal_block",
    )(frame, tokens, moved, mod, *weights)


def join_kernel(offsets, frame_ref, *refs):
    positions = refs[0].shape[0]
    for offset, ref in zip(offsets, refs[:-1]):
        refs[-1][pl.ds(frame_start(frame_ref, offset, positions), positions), :] = ref[...]


def join_frames(frame, pieces, offsets):
    positions, width = pieces[0].shape
    return pl.pallas_call(
        lambda *refs: join_kernel(offsets, *refs),
        out_shape=jax.ShapeDtypeStruct((positions * len(pieces), width), jnp.bfloat16),
        in_specs=[pl.BlockSpec(memory_space=pltpu.SMEM)]
        + [pl.BlockSpec(memory_space=pltpu.VMEM)] * len(pieces),
        compiler_params=pltpu.CompilerParams(vmem_limit_bytes=VMEM_LIMIT),
        cost_estimate=SMALL,
        name="join_frames",
    )(frame, *pieces)


def swap(array, offset, count):
    return lax.ppermute(array, "patch", [(rank, rank ^ offset) for rank in range(count)])


def frame_swap(array, offset, count):
    return lax.ppermute(array, "frame", [(rank, rank ^ offset) for rank in range(count)])


def ring_step(array, frame_count, patch_count):
    order = list(range(0, frame_count, 2)) + list(range(1, frame_count, 2))[::-1]
    pairs = []
    for place, frame in enumerate(order):
        right, left = order[(place + 1) % frame_count], order[place - 1]
        for patch in range(patch_count):
            target = left if patch % 2 else right
            pairs.append((frame * patch_count + patch, target * patch_count + patch))
    return lax.ppermute(array, ("frame", "patch"), pairs)


def make_shards(frame_count, patch_count):
    def hop(array):
        return ring_step(array, frame_count, patch_count)

    def over_cores(array):
        return swap(array, 1, patch_count)

    def exchange(tokens):
        pieces = tokens.reshape(frame_count, -1, tokens.shape[-1])
        pieces = lax.all_to_all(pieces, "frame", 0, 0, tiled=True)
        return pieces.reshape(tokens.shape)

    def shards(
        hidden_states,
        mod_spatial,
        w_spatial_qkv,
        w_spatial_out,
        mod_temporal,
        w_temporal_qkv,
        w_temporal_out,
    ):
        _, patches, width = hidden_states.shape
        barrier = lax.optimization_barrier
        near = range(2, patch_count, 2)
        steps = frame_count // 2
        patch = lax.axis_index("patch").astype(jnp.int32)
        place = ((patch ^ (patch >> 1)) & 1).reshape(1)
        frame = lax.axis_index("frame").astype(jnp.int32).reshape(1)
        place, frame, hidden_states = barrier((place, frame, hidden_states))
        tokens = hidden_states.reshape(patches, width)
        w_qkv = w_spatial_qkv.T

        gathered = [tokens] * patch_count
        for offset in near:
            gathered[offset] = swap(tokens, offset, patch_count)
        gathered[1] = swap(tokens, 1, patch_count)
        weights = list(pack(place, w_temporal_qkv.T, w_temporal_out))
        first = [hop(array) for array in weights]
        other_out = over_cores(w_spatial_out)
        qkv = [None] * patch_count
        for offset in range(2):
            qkv[offset] = spatial_qkv(gathered[offset], mod_spatial, w_qkv)
        qkv[:2] = barrier(qkv[:2])
        gathered, qkv[:2] = barrier((gathered, qkv[:2]))

        for offset in near:
            gathered[offset + 1] = over_cores(gathered[offset])
        qkv[2] = spatial_qkv(gathered[2], mod_spatial, w_qkv, MEDIUM)
        qkv[2], first[0] = barrier((qkv[2], first[0]))

        second = [hop(first[0])]
        for offset in range(3, patch_count):
            qkv[offset] = spatial_qkv(gathered[offset], mod_spatial, w_qkv)
        qkv, other_out = barrier((qkv, other_out))

        qv, keys = zip(*qkv)
        heads = [None] * patch_count
        for offset in near:
            heads[offset + 1] = spatial_attention(qv[offset + 1], qv, keys)
        heads, qv, keys, first = barrier((heads, qv, keys, first))
        second += [hop(array) for array in first[1:]]

        for offset in near:
            heads[offset + 1] = over_cores(heads[offset + 1])
            heads[offset] = spatial_attention(qv[offset], qv, keys)
        partials = [
            chip_partial(heads[offset], heads[offset + 1], w_spatial_out, other_out)
            for offset in near
        ]
        partials, qv, keys = barrier((partials, qv, keys))

        partials = [swap(partial, offset, patch_count) for partial, offset in zip(partials, near)]
        heads[1] = spatial_attention(qv[1], qv, keys)
        heads[1], qv, keys, second[0], first = barrier((heads[1], qv, keys, second[0], first))

        third = hop(second[0])
        heads[0] = spatial_attention(qv[0], qv, keys)
        heads[:2] = barrier(heads[:2])

        heads[1] = over_cores(heads[1])
        base = spatial_base(tokens, mod_spatial, heads[0], heads[1], w_spatial_out, other_out)
        base, first, second[0] = barrier((base, first, second[0]))

        after_spatial = spatial_add(base, mod_spatial, partials)
        after_spatial, third = barrier((after_spatial, third))

        fourth = hop(third)
        if len(first) == 2:
            third_far = swap(third, 2, patch_count)
        arrived = exchange(after_spatial)
        moved = temporal_norm(arrived, mod_temporal, patches // frame_count)
        weights += first
        others = [over_cores(array) for array in first]
        rest = second + [third]
        if len(first) == 2:
            rest += [third_far, fourth]
        else:
            for _ in range(4, steps):
                rest.append(fourth)
                fourth = hop(fourth)
            weights.append(fourth)
        for array in rest:
            others += [array, over_cores(array)]
        weights += others
        positions = patches // frame_count
        pieces = list(temporal_block(frame, arrived, moved, mod_temporal, weights, positions))
        middle = frame_count // 2
        order = [1, middle, 2, *range(middle + 1, frame_count), *range(3, middle)]
        order = [0, *dict.fromkeys(order)]
        for offset in order[1:]:
            pieces[offset] = frame_swap(pieces[offset], offset, frame_count)
        result = join_frames(frame, [pieces[offset] for offset in order], order)
        return result.reshape(1, patches, width)

    return shards


def solution(mesh):
    in_specs = (
        P("frame", "patch", None),
        P(),
        P(None, "patch"),
        P("patch", None),
        P(),
        P(None, "frame"),
        P("frame", None),
    )
    out_specs = P("frame", "patch", None)
    shards = make_shards(mesh.shape["frame"], mesh.shape["patch"])
    return jax.shard_map(shards, mesh=mesh, in_specs=in_specs, out_specs=out_specs, check_vma=False)
```
